256 devices in a mesh: blk: 32 (over x_lo, z, core), rep: 8 (over x_hi, y).
Axes of the slice: x: 4 (x_hi: 2, x_lo: 2; x = x_hi * 2 + x_lo), y: 4, z: 8, core: 2. Of those that a mesh axis runs over, the one named last changes fastest.
Arguments:
- node_features: bfloat16 [65536, 128], P(('blk', 'rep')), may hold values from -6 to 6
- weight_matrix: bfloat16 [128, 512], replicated, may hold values from -0.5 to 0.5
- bias_vector: float32 [512], replicated, may hold values from -3 to 3
- node_degree: int32 [65536], P(('blk', 'rep')), may hold values from 4 to 64, as said below
- tile_values: bfloat16 [32, 8, 64, 2, 128, 128], P('blk', 'rep'), may hold values from 0 to 1
- tile_row: int32 [32, 8, 64, 2], P('blk', 'rep'), may hold values from 0 to 15
- tile_count: int32 [32, 8, 64], P('blk', 'rep'), may hold values from 1 to 2
- cotangent: bfloat16 [65536, 512], P(('blk', 'rep')), may hold values from -6 to 6
Outputs:
- hidden_out: bfloat16 [65536, 512], P(('blk', 'rep'))
- weight_grad: float32 [128, 512], replicated
- input_grad: bfloat16 [65536, 128], P(('blk', 'rep'))
The draws below stay inside these ranges and needn't reach their ends.
Inputs may be any that keep to these rules, and one draw needn't show every extreme that they name: `tile_row`: row tile of a slot, within the 2048 rows of its group. `tile_count`: number of live slots of a column tile; slots at or past it are ignored. `node_degree`: degree of a node, one of 4, 16 and 64.
All inputs are finite; a program needn't handle non-finite values.
Results may differ from the reference program's by a relative error of at most 0.0027.
Values may be sent and summed in bfloat16 or wider, within the bound.
No kernel may reach another device: no remote copies, remote signals or barrier semaphores. Data moves between devices by JAX's collectives and lax.ppermute only.
A program may use at most 128 MiB of HBM per device.

```python
import math
import jax
import jax.numpy as jnp
from jax import lax

F_IN = 128
F_OUT = 512
TILE = 128
CAP = 2
ROWS_DEV = 256
NODES = 65536
NCT = 64
ROWT = 16
N_BLK = 32
N_REP = 8


def draw_node_degree(key, part):
    key = jax.random.fold_in(key, 7)
    power = jax.random.randint(key, (NODES,), 1, 4)
    return jnp.left_shift(jnp.int32(1), 2 * power).astype(jnp.int32)


def with_ends(entries, own_key, low, high):
    spot = [jax.random.randint(jax.random.fold_in(own_key, axis), (), 0, length) for axis, length in enumerate(entries.shape)]
    longest = entries.shape.index(max(entries.shape))
    next_to = spot[:longest] + [(spot[longest] + 1) % entries.shape[longest]] + spot[longest + 1:]
    return entries.at[tuple(spot)].set(low).at[tuple(next_to)].set(high)


def block_levels(own_key, extent, split, least, largest):
    gain, own = 1.0, jax.random.fold_in(own_key, 6)
    for dim, blocks in split:
        steps = jnp.exp(jax.random.uniform(jax.random.fold_in(own, dim), (blocks,), jnp.float32, least / len(split), largest / len(split)))
        gain = gain * jnp.repeat(steps, extent[dim] // blocks).reshape([-1 if axis == dim else 1 for axis in range(len(extent))])
    return gain


def bell_draw(stream_key, shape, deviation, reach, cuts=(), held_as=jnp.bfloat16):
    level = block_levels(stream_key, shape, cuts, -0.22, 0.18) if cuts else 1.0
    drawn = jax.random.normal(stream_key, shape, jnp.float32) * deviation * level
    return jnp.minimum(jnp.maximum(drawn, -reach), reach).astype(held_as)


def setup_inputs(seed: int = 0) -> dict:
    seeds = jax.random.split(jax.random.key(seed), 9)
    node_features = bell_draw(seeds[0], (NODES, F_IN), 1.0, 6.0, ((0, 256),))
    weight_matrix = bell_draw(seeds[1], (F_IN, F_OUT), F_IN ** -0.5, 0.5)
    bias_vector = bell_draw(seeds[2], (F_OUT,), 0.5, 3.0, (), jnp.float32)
    node_degree = draw_node_degree(jax.random.fold_in(seeds[8], 71), 0)
    tile_values = jnp.clip(1.0 * jax.random.uniform(seeds[4], (N_BLK, N_REP, NCT, CAP, TILE, TILE), jnp.float32) ** block_levels(seeds[4], (N_BLK, N_REP, NCT, CAP, TILE, TILE), ((0, 32), (1, 8)), -0.2, 0.2), 0.0, 1.0).astype(jnp.bfloat16)
    tile_row = with_ends(jax.random.randint(seeds[5], (N_BLK, N_REP, NCT, CAP), 0, ROWT), jax.random.fold_in(seeds[5], 1), 0, ROWT - 1).astype(jnp.int32)
    tile_count = with_ends(jax.random.randint(seeds[6], (N_BLK, N_REP, NCT), 1, CAP + 1), jax.random.fold_in(seeds[6], 1), 1, CAP).astype(jnp.int32)
    cotangent = bell_draw(seeds[7], (NODES, F_OUT), 1.0, 6.0, ((0, 256),))
    return {"node_features": node_features, "weight_matrix": weight_matrix, "bias_vector": bias_vector, "node_degree": node_degree, "tile_values": tile_values, "tile_row": tile_row, "tile_count": tile_count, "cotangent": cotangent}


exact_mode = lax.Precision.HIGHEST

def gelu_tanh(values):
    return jax.nn.gelu(values, approximate=True)

def slot_weights(slot_rows, live_slots, row_tiles):
    slot_ids = lax.broadcasted_iota(jnp.int32, slot_rows.shape, 1)
    alive = slot_ids < live_slots[:, None]
    targets = lax.broadcasted_iota(jnp.int32, slot_rows.shape + (row_tiles,), 2)
    return ((slot_rows[:, :, None] == targets) & alive[:, :, None]).astype(jnp.float32)

def reference(node_features, weight_matrix, bias_vector, node_degree, tile_values, tile_row, tile_count, cotangent):
    row_tiles = N_REP * ROWS_DEV // TILE
    row_scale = 1.0 / jnp.sqrt(node_degree.astype(jnp.float32))
    scaled_low = (node_features.astype(jnp.float32) * row_scale[:, None]).astype(jnp.bfloat16)
    scaled_in = lax.optimization_barrier(scaled_low).astype(jnp.float32)
    columns = scaled_in.reshape(N_BLK, N_REP, ROWS_DEV, F_IN)

    def group_forward(block_index):

        def one_replica(replica):
            tile_block = tile_values[block_index, replica].astype(jnp.float32)
            weights = slot_weights(tile_row[block_index, replica], tile_count[block_index, replica], row_tiles)
            column_part = lax.dynamic_index_in_dim(columns, replica, 1, keepdims=False).reshape(N_BLK * ROWS_DEV // TILE, TILE, F_IN)
            products = jnp.einsum('kscj,kjf->kscf', tile_block, column_part, precision=exact_mode)
            return jnp.einsum('ksr,kscf->rcf', weights, products, precision=exact_mode)
        return lax.optimization_barrier(jnp.sum(jax.vmap(one_replica)(jnp.arange(N_REP)), axis=0))
    aggregated = lax.map(group_forward, jnp.arange(N_BLK)).reshape(NODES, F_IN)
    weight_wide = weight_matrix.astype(jnp.float32)
    pre_act = row_scale[:, None] * jnp.dot(aggregated, weight_wide, precision=exact_mode) + bias_vector[None, :]
    activated, pullback = jax.vjp(gelu_tanh, pre_act)
    pre_grad = pullback(cotangent.astype(jnp.float32))[0]
    weight_grad = jnp.dot(node_features.astype(jnp.float32).T, pre_grad, precision=exact_mode) * (1.0 / math.sqrt(NODES))
    back_wide = row_scale[:, None] * pre_grad
    back_rows = jnp.dot(back_wide, weight_wide.T, precision=exact_mode)
    grouped = back_rows.reshape(N_BLK, row_tiles, TILE, F_IN)

    def group_backward(carried, block_index):
        group_part = lax.dynamic_index_in_dim(grouped, block_index, 0, keepdims=False)

        def one_replica(replica):
            tile_block = tile_values[block_index, replica].astype(jnp.float32)
            weights = slot_weights(tile_row[block_index, replica], tile_count[block_index, replica], row_tiles)
            picked = jnp.einsum('ksr,rcf->kscf', weights, group_part, precision=exact_mode)
            terms = jnp.einsum('kscj,kscf->kjf', tile_block, picked, precision=exact_mode)
            return terms.reshape(N_BLK, ROWS_DEV, F_IN)
        spread_terms = jax.vmap(one_replica)(jnp.arange(N_REP))
        return (carried + jnp.transpose(spread_terms, (1, 0, 2, 3)), None)
    start_acc = jnp.zeros((N_BLK, N_REP, ROWS_DEV, F_IN), jnp.float32)
    accumulated, _ = lax.scan(group_backward, start_acc, jnp.arange(N_BLK))
    input_grad = row_scale[:, None] * accumulated.reshape(NODES, F_IN)
    return (activated.astype(jnp.bfloat16), weight_grad, input_grad.astype(jnp.bfloat16))
```

```python
import functools

import jax
import jax.numpy as jnp
from jax import lax
from jax.experimental import pallas as pl
from jax.experimental.pallas import tpu as pltpu
from jax.sharding import PartitionSpec as P

f32, bf16, f16 = jnp.float32, jnp.bfloat16, jnp.float16

TILE = 128
OWN = 256
BLOCK = OWN + 16
N_X, N_Z, N_C = 2, 8, 2
N_Y = 4
SLOTS = 2
ROW_TILES = 16
VMEM_LIMIT = 40 * 1024 * 1024
DISTANCES = (1, 2, 3)


def blk_index(x, z, c):
    return (x * N_Z + z) * N_C + c


def permute_blk(value, move):
    pairs = []
    for x in range(N_X):
        for z in range(N_Z):
            for c in range(N_C):
                pairs.append((blk_index(x, z, c), blk_index(*move(x, z, c))))
    return lax.ppermute(value, "blk", pairs)


def to_core(x, z, c):
    return x, z, 1 - c


def to_x(x, z, c):
    return 1 - x, z, c


def to_z(distance):
    return lambda x, z, c: (x, (z + distance) % N_Z, c)


def to_z_by_core(distance):
    return lambda x, z, c: (x, (z + (distance if c == 0 else -distance)) % N_Z, c)


def to_z_xor(bit):
    return lambda x, z, c: (x, z ^ bit, c)


def exponent_above(largest):
    return jnp.ceil(jnp.log2(jnp.maximum(largest, 1e-30))) + 1.0


def as_column(row):
    n = row.shape[1]
    diagonal = lax.broadcasted_iota(jnp.int32, (n, n), 0) == lax.broadcasted_iota(
        jnp.int32, (n, n), 1
    )
    return jnp.sum(jnp.where(diagonal, row, 0.0), axis=1, keepdims=True)


def scale_of(degree):
    scale = 1.0 / jnp.sqrt(degree.astype(f32))
    rows = [scale[i : i + 1, :] for i in range(scale.shape[0])]
    return jnp.concatenate(rows, 1), jnp.concatenate([as_column(r) for r in rows], 0)


def split(value):
    high = value.astype(bf16)
    return high, (value - high.astype(f32)).astype(bf16)


def scale_kernel(features_ref, degree_ref, cot_ref, own_ref):
    _, column = scale_of(degree_ref[...])
    scaled = (features_ref[...].astype(f32) * column).astype(bf16)
    own_ref[:OWN, :] = scaled
    cot = jnp.max(jnp.abs(cot_ref[...].astype(f32)))
    feature = jnp.max(jnp.abs(scaled.astype(f32)))
    rows = lax.broadcasted_iota(jnp.int32, (BLOCK - OWN, TILE), 0)
    own_ref[OWN:, :] = jnp.where(rows < 8, cot, feature).astype(bf16)


def forward_kernel(place_ref, rows_ref, count_ref, tiles_ref, *refs):
    pieces, out_ref, acc_ref = refs[:-2], refs[-2], refs[-1]
    x, z, c = place_ref[0], place_ref[1], place_ref[2]
    acc_ref[...] = jnp.zeros_like(acc_ref)
    largest = None
    for ref, blocks in zip(pieces, forward_order(), strict=True):
        for at, (dx, dz, dc) in enumerate(blocks):
            column_block = blk_index(x ^ dx, lax.rem(z + place_ref[3 + dz], N_Z), c ^ dc)
            marks = ref[at, OWN:, :]
            largest = marks if largest is None else jnp.maximum(largest, marks)
            for half in range(OWN // TILE):
                k = column_block * (OWN // TILE) + half
                part = ref[at, half * TILE : (half + 1) * TILE, :]
                product = jnp.dot(tiles_ref[k], part, preferred_element_type=f32)
                for slot in range(SLOTS):
                    row = rows_ref[k * SLOTS + slot]
                    row = jnp.where(slot < count_ref[k], row, ROW_TILES)
                    where = pl.ds(pl.multiple_of(row * TILE, TILE), TILE)
                    acc_ref[where, :] += product[slot * TILE : (slot + 1) * TILE, :]
    marks = exponent_above(largest.astype(f32))
    shrink = 2.0 * jnp.exp2(-marks[8:9, :])
    for r in range(out_ref.shape[0]):
        out_ref[r, :OWN, :] = acc_ref[r * OWN : (r + 1) * OWN, :] * shrink
        out_ref[r, OWN:, :] = marks


def forward_order():
    own = [[(0, 0, 0), (0, 0, 1)], [(1, 0, 0), (1, 0, 1)]]
    for i in (1, 2, 3):
        own.append([(0, i, 0), (0, i, 1)])
        own.append([(1, i, 0), (1, i, 1)])
        own.append([(0, i + 4, 1), (0, i + 4, 0), (1, i + 4, 1), (1, i + 4, 0)])
    own.append([(0, 4, 0)])
    own.append([(1, 4, 0)])
    own.append([(0, 4, 1), (1, 4, 1)])
    return own


def middle_kernel(
    parts_ref,
    weight_ref,
    bias_ref,
    degree_ref,
    features_ref,
    cot_ref,
    hidden_ref,
    back_ref,
    grad_ref,
    factor_ref,
):
    row_scale, column_scale = scale_of(degree_ref[...])
    summed = jnp.zeros((OWN, TILE), f32)
    cot_mark = feature_mark = None
    for r in range(parts_ref.shape[0]):
        cot_r, feature_r = parts_ref[r, OWN : OWN + 1, :], parts_ref[r, OWN + 8 : OWN + 9, :]
        summed += parts_ref[r, :OWN, :] * (0.5 * jnp.exp2(feature_r))
        cot_mark = cot_r if cot_mark is None else jnp.maximum(cot_mark, cot_r)
        feature_mark = feature_r if feature_mark is None else jnp.maximum(feature_mark, feature_r)
    weight = weight_ref[...]
    high, low = split(summed)
    mixed = jnp.dot(high, weight, preferred_element_type=f32)
    mixed += jnp.dot(low, weight, preferred_element_type=f32)
    pre = column_scale * mixed + bias_ref[...]
    root = 0.7978845608028654
    square = pre * pre
    bent = jnp.tanh(root * pre * (1.0 + 0.044715 * square))
    half_up = 0.5 * (1.0 + bent)
    hidden_ref[...] = (pre * half_up).astype(bf16)
    slope = half_up + 0.5 * pre * (1.0 - bent * bent) * (root * (1.0 + 0.134145 * square))
    shrink = jnp.exp2(-cot_mark[:, :1])
    grad = cot_ref[...].astype(f32) * shrink * slope
    high, low = split(grad)
    across = (((1,), (1,)), ((), ()))
    back = lax.dot_general(weight, high, across, preferred_element_type=f32)
    back += lax.dot_general(weight, low, across, preferred_element_type=f32)
    weight_mark = exponent_above(jnp.max(jnp.abs(weight.astype(f32)), axis=(0, 1), keepdims=True))
    back_ref[...] = back * row_scale * (64.0 * jnp.exp2(-weight_mark))
    down = (((0,), (0,)), ((), ()))
    features = features_ref[...]
    local = lax.dot_general(features, high, down, preferred_element_type=f32)
    local += lax.dot_general(features, low, down, preferred_element_type=f32)
    local = local * (16.0 * jnp.exp2(-feature_mark[:, :1]))
    for r in range(grad_ref.shape[0]):
        i, j = r // 2, r % 2
        grad_ref[r] = local[i * 32 : (i + 1) * 32, j * 256 : (j + 1) * 256]
    one = jnp.ones((8, TILE), f32)
    factor_ref[0] = one * (16.0 * jnp.exp2(cot_mark + weight_mark))
    factor_ref[1] = one * (jnp.exp2(cot_mark + feature_mark) / 4096.0)


def backward_kernel(place_ref, rows_ref, count_ref, tiles_ref, back_ref, keep_ref, give_ref, group_ref):
    x, z, c = place_ref[0], place_ref[1], place_ref[2]
    for r in range(ROW_TILES):
        value = back_ref[r // 2, :, (r % 2) * TILE : (r % 2 + 1) * TILE] * (1.0 / 1024.0)
        high, low = split(value)
        group_ref[r, :TILE, :] = high
        group_ref[r, TILE:, :] = low
    group_ref[ROW_TILES] = jnp.zeros(group_ref.shape[1:], bf16)
    for dc, ref in ((1, give_ref), (0, keep_ref)):
        for at, (dx, shift) in enumerate(backward_order()):
            column_block = blk_index(x ^ dx, lax.rem(z + shift, N_Z), c ^ dc)
            for half in range(OWN // TILE):
                k = column_block * (OWN // TILE) + half
                picked = []
                for slot in range(SLOTS):
                    row = rows_ref[k * SLOTS + slot]
                    picked.append(group_ref[jnp.where(slot < count_ref[k], row, ROW_TILES)])
                both = jnp.dot(
                    jnp.concatenate(picked, 1), tiles_ref[k], preferred_element_type=f32
                )
                ref[at, :, half * TILE : (half + 1) * TILE] = both[:TILE] + both[TILE:]


Z_ORDER = (4, 3, 5, 2, 6, 1, 7, 0)


def backward_order():
    return [(dx, shift) for dx in (1, 0) for shift in Z_ORDER]


SMEM = pl.BlockSpec(memory_space=pltpu.SMEM)
VMEM = pl.BlockSpec(memory_space=pltpu.VMEM)


def shape(dims, dtype):
    return jax.ShapeDtypeStruct(dims, dtype)


def call(kernel, outs, smem, vmem, scratch=(), cost=0):
    return pl.pallas_call(
        kernel,
        out_shape=outs,
        in_specs=[SMEM] * smem + [VMEM] * vmem,
        out_specs=jax.tree.map(lambda _: VMEM, outs),
        scratch_shapes=list(scratch),
        compiler_params=pltpu.CompilerParams(vmem_limit_bytes=VMEM_LIMIT),
        cost_estimate=pl.CostEstimate(flops=cost, bytes_accessed=4 << 20, transcendentals=0),
    )


def gather_blocks(own):
    own = own[None]
    pair = jnp.concatenate([own, permute_blk(own, to_core)])
    far = permute_blk(own, to_z_by_core(4))
    near = [permute_blk(pair, to_z_by_core(d)) for d in (3, 2, 1)][::-1]
    pieces = [pair, permute_blk(pair, to_x)]
    for got in near:
        other = permute_blk(got, to_x)
        pieces += [got, other, permute_blk(jnp.concatenate([got, other]), to_core)]
    other = permute_blk(far, to_x)
    pieces += [far, other, permute_blk(jnp.concatenate([far, other]), to_core)]
    return pieces


def scatter_terms(keep, give):
    got = permute_blk(give.astype(f16), to_core)
    chip = keep + got.astype(f32)
    total = None
    for i, shift in enumerate(Z_ORDER):
        term = chip[N_Z + i] + permute_blk(chip[i].astype(f16), to_x).astype(f32)
        if shift:
            term = permute_blk(term.astype(f16), to_z(shift)).astype(f32)
        total = term if total is None else total + term
    return total


def per_device(
    node_features,
    weight_matrix,
    bias_vector,
    node_degree,
    tile_values,
    tile_row,
    tile_count,
    cotangent,
):
    n_out = weight_matrix.shape[1]
    tiles = tile_values.reshape(-1, SLOTS * TILE, TILE)
    rows = tile_row.reshape(-1)
    count = tile_count.reshape(-1)
    degree = node_degree.reshape(OWN // TILE, TILE)
    at = lax.axis_index("blk")
    x, z, c = at // (N_Z * N_C), at // N_C % N_Z, at % N_C
    up = [d % N_Z for d in (0, -1, -2, -3, 4, 1, 2, 3)]
    down = [-d % N_Z for d in up]
    place = jnp.concatenate(
        [jnp.stack([x, z, c]), jnp.where(c == 0, jnp.array(up), jnp.array(down))]
    ).astype(jnp.int32)

    own = call(scale_kernel, shape((BLOCK, TILE), bf16), 0, 3)(node_features, degree, cotangent)
    pieces = gather_blocks(own)
    partial = call(
        forward_kernel,
        shape((8, BLOCK, TILE), f32),
        3,
        1 + len(pieces),
        [pltpu.VMEM(((ROW_TILES + 1) * TILE, TILE), f32)],
        cost=1 << 29,
    )(place, rows, count, tiles, *pieces)
    parts = lax.all_to_all(partial.astype(f16), "rep", 0, 0).astype(f32)
    hidden, back, grad, factor = call(
        middle_kernel,
        (
            shape((OWN, n_out), bf16),
            shape((TILE, OWN), f32),
            shape((8, 32, 256), f32),
            shape((2, 8, TILE), f32),
        ),
        0,
        6,
        cost=1 << 27,
    )(parts, weight_matrix, bias_vector.reshape(1, -1), degree, node_features, cotangent)

    sent = jnp.concatenate([jnp.broadcast_to(back[None], (8, TILE, OWN)), grad], 1).astype(f16)
    got = lax.all_to_all(sent, "rep", 0, 0).astype(f32)
    keep, give = call(
        backward_kernel,
        (shape((16, TILE, OWN), f32), shape((16, TILE, OWN), f32)),
        3,
        2,
        [pltpu.VMEM((ROW_TILES + 1, 2 * TILE, TILE), bf16)],
        cost=1 << 30,
    )(place, rows, count, tiles, got[:, :TILE])
    total = scatter_terms(keep, give)
    row_scale = 1.0 / jnp.sqrt(node_degree.astype(f32))
    input_grad = ((total * row_scale[None, :]).T * factor[0, :1, :]).astype(bf16)

    grad = jnp.sum(got[:, TILE:], 0)
    for move in (to_core, to_x, to_z_xor(1), to_z_xor(2), to_z_xor(4)):
        grad = grad + permute_blk(grad, move)
    whole = lax.all_to_all(jnp.broadcast_to(grad[None], (8, 32, 256)), "rep", 0, 0)
    weight_grad = whole.reshape(4, 2, 32, 256).transpose(0, 2, 1, 3).reshape(TILE, n_out)
    weight_grad = weight_grad * factor[1, 0, 0]
    return hidden, weight_grad, input_grad


def solution(mesh):
    in_specs = (
        P(("blk", "rep"), None),
        P(),
        P(),
        P(("blk", "rep")),
        P("blk", "rep", None, None, None, None),
        P("blk", "rep", None, None),
        P("blk", "rep", None),
        P(("blk", "rep"), None),
    )
    out_specs = (P(("blk", "rep"), None), P(), P(("blk", "rep"), None))
    return jax.shard_map(
        per_device, mesh=mesh, in_specs=in_specs, out_specs=out_specs, check_vma=False
    )
```

```python
import functools

import jax
import jax.numpy as jnp
from jax import lax
from jax.experimental import pallas as pl
from jax.experimental.pallas import tpu as pltpu
from jax.sharding import PartitionSpec as P

f32, bf16, f16 = jnp.float32, jnp.bfloat16, jnp.float16

TILE = 128
OWN = 256
BLOCK = OWN + 16
N_X, N_Z, N_C = 2, 8, 2
N_Y = 4
SLOTS = 2
ROW_TILES = 16
VMEM_LIMIT = 16 * 1024 * 1024


def blk_index(x, z, c):
    return (x * N_Z + z) * N_C + c


def permute_blk(value, move):
    pairs = []
    for x in range(N_X):
        for z in range(N_Z):
            for c in range(N_C):
                pairs.append((blk_index(x, z, c), blk_index(*move(x, z, c))))
    return lax.ppermute(value, "blk", pairs)


def to_core(x, z, c):
    return x, z, 1 - c


def to_x(x, z, c):
    return 1 - x, z, c


def to_z_by_core(distance):
    return lambda x, z, c: (x, (z + (distance if c == 0 else -distance)) % N_Z, c)


def exponent_above(largest):
    return jnp.ceil(jnp.log2(jnp.maximum(largest, 1e-30))) + 1.0


def as_column(row):
    n = row.shape[1]
    diagonal = lax.broadcasted_iota(jnp.int32, (n, n), 0) == lax.broadcasted_iota(
        jnp.int32, (n, n), 1
    )
    return jnp.sum(jnp.where(diagonal, row, 0.0), axis=1, keepdims=True)


def scale_of(degree):
    scale = 1.0 / jnp.sqrt(degree.astype(f32))
    rows = [scale[i : i + 1, :] for i in range(scale.shape[0])]
    return jnp.concatenate(rows, 1), jnp.concatenate([as_column(r) for r in rows], 0)


def split(value):
    high = value.astype(bf16)
    return high, (value - high.astype(f32)).astype(bf16)


def scale_kernel(features_hbm, degree_hbm, cot_hbm, own_ref, features_ref, degree_ref, cot_ref, sems):
    copies = [
        pltpu.make_async_copy(src, dst, sems.at[i])
        for i, (src, dst) in enumerate(
            [(degree_hbm, degree_ref), (features_hbm, features_ref), (cot_hbm, cot_ref)]
        )
    ]
    for copy in copies:
        copy.start()
    copies[0].wait()
    _, column = scale_of(degree_ref[...])
    copies[1].wait()
    scaled = (features_ref[...].astype(f32) * column).astype(bf16)
    own_ref[0, :OWN, :] = scaled
    copies[2].wait()
    cot = jnp.max(jnp.abs(cot_ref[...].astype(f32)))
    feature = jnp.max(jnp.abs(scaled.astype(f32)))
    rows = lax.broadcasted_iota(jnp.int32, (BLOCK - OWN, TILE), 0)
    own_ref[0, OWN:, :] = jnp.where(rows < 8, cot, feature).astype(bf16)
    own_ref[1] = own_ref[0]


def column_block(at, dx, dz, dc):
    x, z, c = at // (N_Z * N_C), at // N_C % N_Z, at % N_C
    z = (z + N_Z + (1 - 2 * c) * dz) % N_Z
    return blk_index(x + dx - 2 * dx * x, z, c + dc - 2 * dc * c)


def add_products(order, place_ref, rows_ref, count_ref, tiles_ref, pieces, acc_ref):
    column_blocks = [
        column_block(place_ref[0], *block) for blocks in order for block in blocks
    ]
    refs = [(ref, at) for ref, blocks in zip(pieces, order, strict=True) for at in range(len(blocks))]
    largest = None
    for i, (ref, at) in enumerate(refs):
        marks = ref[at, OWN:, :].astype(f32)
        largest = marks if largest is None else jnp.maximum(largest, marks)
        for half in range(OWN // TILE):
            k = column_blocks[i] * (OWN // TILE) + half
            part = ref[at, half * TILE : (half + 1) * TILE, :]
            product = jnp.dot(tiles_ref[k], part, preferred_element_type=f32)
            for slot in range(SLOTS):
                row = rows_ref[k * SLOTS + slot]
                row = jnp.where(slot < count_ref[k], row, ROW_TILES)
                where = pl.ds(pl.multiple_of(row * TILE, TILE), TILE)
                acc_ref[where, :] += product[slot * TILE : (slot + 1) * TILE, :]
    return largest


def forward_kernel(order, place_ref, rows_ref, count_ref, tiles_ref, *refs):
    (acc_ref, marks_ref), refs = refs[-2:], refs[:-2]
    pieces = refs[-len(order) :]
    if len(refs) > len(order):
        acc_ref[...] = refs[0][...]
    else:
        acc_ref[...] = jnp.zeros_like(acc_ref)
    marks = add_products(order, place_ref, rows_ref, count_ref, tiles_ref, pieces, acc_ref)
    if len(refs) > len(order):
        marks = jnp.maximum(marks, refs[1][...])
    marks_ref[...] = marks


def forward_last_kernel(place_ref, rows_ref, count_ref, tiles_ref, begun_ref, begun_marks, *refs):
    pieces, (out_ref, acc_ref) = refs[:-2], refs[-2:]
    acc_ref[...] = begun_ref[...]
    largest = add_products(
        LAST_ORDER, place_ref, rows_ref, count_ref, tiles_ref, pieces, acc_ref
    )
    marks = exponent_above(jnp.maximum(largest, begun_marks[...]))
    shrink = 2.0 * jnp.exp2(-marks[8:9, :])
    for r in range(out_ref.shape[0]):
        out_ref[r, :OWN, :] = acc_ref[r * OWN : (r + 1) * OWN, :] * shrink
        out_ref[r, OWN:, :] = marks


FORWARD_ORDERS = [
    [[(0, 0, 0), (0, 0, 1)]],
    [[(1, 0, 0), (1, 0, 1)], [(0, -1, 0), (0, -1, 1), (0, -2, 0), (0, -2, 1)]],
    [[(1, -1, 0), (1, -1, 1), (1, -2, 0), (1, -2, 1)], [(0, -3, 0), (0, -3, 1), (0, 4, 0)]],
    [
        [(dx, i, dc) for dx in (0, 1) for i in (1, 2) for dc in (1, 0)],
        [(1, -3, 0), (1, -3, 1), (1, 4, 0)],
        [(0, 3, 1), (0, 3, 0), (0, 4, 1)],
    ],
]
LAST_ORDER = [[(1, 3, 1), (1, 3, 0), (1, 4, 1)]]


def middle_kernel(
    parts_ref,
    weight_ref,
    bias_ref,
    degree_ref,
    features_ref,
    cot_ref,
    hidden_ref,
    back_ref,
    grad_ref,
    factor_ref,
):
    row_scale, column_scale = scale_of(degree_ref[...])
    summed = jnp.zeros((OWN, TILE), f32)
    cot_mark = feature_mark = None
    for r in range(parts_ref.shape[0]):
        cot_r, feature_r = parts_ref[r, OWN : OWN + 1, :], parts_ref[r, OWN + 8 : OWN + 9, :]
        summed += parts_ref[r, :OWN, :] * (0.5 * jnp.exp2(feature_r))
        cot_mark = cot_r if cot_mark is None else jnp.maximum(cot_mark, cot_r)
        feature_mark = feature_r if feature_mark is None else jnp.maximum(feature_mark, feature_r)
    weight = weight_ref[...]
    high, low = split(summed)
    mixed = jnp.dot(high, weight, preferred_element_type=f32)
    mixed += jnp.dot(low, weight, preferred_element_type=f32)
    pre = column_scale * mixed + bias_ref[...]
    root = 0.7978845608028654
    square = pre * pre
    bent = jnp.tanh(root * pre * (1.0 + 0.044715 * square))
    half_up = 0.5 * (1.0 + bent)
    hidden_ref[...] = (pre * half_up).astype(bf16)
    slope = half_up + 0.5 * pre * (1.0 - bent * bent) * (root * (1.0 + 0.134145 * square))
    shrink = jnp.exp2(-cot_mark[:, :1])
    grad = cot_ref[...].astype(f32) * shrink * slope
    high, low = split(grad)
    across = (((1,), (1,)), ((), ()))
    back = lax.dot_general(weight, high, across, preferred_element_type=f32)
    back += lax.dot_general(weight, low, across, preferred_element_type=f32)
    weight_mark = exponent_above(jnp.max(jnp.abs(weight.astype(f32)), axis=(0, 1), keepdims=True))
    back_ref[...] = back * row_scale * (64.0 * jnp.exp2(-weight_mark))
    down = (((0,), (0,)), ((), ()))
    features = features_ref[...]
    local = lax.dot_general(features, high, down, preferred_element_type=f32)
    local += lax.dot_general(features, low, down, preferred_element_type=f32)
    local = local * (0.25 * jnp.exp2(-feature_mark[:, :1]))
    for r in range(grad_ref.shape[0]):
        i, j = r // 2, r % 2
        grad_ref[r] = local[i * 32 : (i + 1) * 32, j * 256 : (j + 1) * 256]
    one = jnp.ones((8, TILE), f32)
    factor_ref[0] = one * (16.0 * jnp.exp2(cot_mark + weight_mark))
    factor_ref[1] = one * (jnp.exp2(cot_mark + feature_mark) / 64.0)


def backward_kernel(orders, place_ref, rows_ref, count_ref, tiles_ref, back_ref, *refs):
    outs, group_ref = refs[:-1], refs[-1]
    for r in range(ROW_TILES):
        value = back_ref[r // 2, :, (r % 2) * TILE : (r % 2 + 1) * TILE] * (1.0 / 1024.0)
        high, low = split(value)
        group_ref[r, :TILE, :] = high
        group_ref[r, TILE:, :] = low
    group_ref[ROW_TILES] = jnp.zeros(group_ref.shape[1:], bf16)
    for ref, order in zip(outs, orders, strict=True):
        for at, block in enumerate(order):
            block = column_block(place_ref[0], *block)
            for half in range(OWN // TILE):
                k = block * (OWN // TILE) + half
                picked = []
                for slot in range(SLOTS):
                    row = rows_ref[k * SLOTS + slot]
                    picked.append(group_ref[jnp.where(slot < count_ref[k], row, ROW_TILES)])
                both = jnp.dot(
                    jnp.concatenate(picked, 1), tiles_ref[k], preferred_element_type=f32
                )
                ref[at, :, half * TILE : (half + 1) * TILE] = both[:TILE] + both[TILE:]


def sum_kernel(place_ref, own_ref, mine_ref, theirs_ref, out_ref):
    z, c = place_ref[0] // N_C % N_Z, place_ref[0] % N_C
    total = None
    for at in range(N_Z):
        below = (z - at + N_Z) % N_Z
        index = jnp.where(below <= 4, below, N_Z - below)
        side = jnp.where(below <= 4, c, 1 - c)
        index = jnp.maximum(index, 1) - 1
        value = jnp.where(side == 0, mine_ref[index], theirs_ref[index])
        value = jnp.where(below == 0, own_ref[...], value)
        total = value if total is None else total + value
    out_ref[...] = total


def assemble_kernel(slices_ref, factor_ref, out_ref):
    factor = jnp.concatenate([factor_ref[1, :1, :]] * 2, 1)
    for r in range(slices_ref.shape[0]):
        i, j = r // 2, r % 2
        out_ref[i * 32 : (i + 1) * 32, j * 256 : (j + 1) * 256] = slices_ref[r] * factor


GIVE_FAR = [(dx, *rest) for dx in (1, 0) for rest in ((4, 1), (-3, 1), (-3, 0))]
GIVE_NEAR = [(dx, *rest) for dx in (1, 0) for rest in ((-2, 1), (-2, 0), (-1, 1), (-1, 0), (0, 1))]
KEEP_FAR = [(dx, *rest) for dx in (1, 0) for rest in ((4, 0), (3, 0), (3, 1))]
KEEP_NEAR = [(dx, *rest) for dx in (1, 0) for rest in ((2, 0), (2, 1), (1, 0), (1, 1), (0, 0))]


SMEM = pl.BlockSpec(memory_space=pltpu.SMEM)
VMEM = pl.BlockSpec(memory_space=pltpu.VMEM)
HBM = pl.BlockSpec(memory_space=pltpu.HBM)


def shape(dims, dtype):
    return jax.ShapeDtypeStruct(dims, dtype)


def call(kernel, outs, ins, scratch=(), cost=0):
    return pl.pallas_call(
        kernel,
        out_shape=outs,
        in_specs=ins,
        out_specs=jax.tree.map(lambda _: VMEM, outs),
        scratch_shapes=list(scratch),
        compiler_params=pltpu.CompilerParams(vmem_limit_bytes=VMEM_LIMIT),
        cost_estimate=pl.CostEstimate(flops=cost, bytes_accessed=1 << 20, transcendentals=0),
    )


def after(value, *others):
    return lax.optimization_barrier((value, *others))[0]


def together(*values):
    return lax.optimization_barrier(values)


def gather_blocks(own, forward):
    pair = lax.dynamic_update_slice(own, permute_blk(own[:1], to_core), (1, 0, 0))
    *begun, pair_x, near_1, near_2 = together(
        *forward(0, pair),
        permute_blk(pair, to_x),
        permute_blk(pair, to_z_by_core(1)),
        permute_blk(pair, to_z_by_core(2)),
    )
    near = jnp.concatenate([near_1, near_2])
    *begun, far, near_x = together(
        *forward(1, *begun, pair_x, near),
        permute_blk(near[:3], to_z_by_core(2)),
        permute_blk(near, to_x),
    )
    *begun, far_core, near_core, far_x = together(
        *forward(2, *begun, near_x, far),
        permute_blk(far, to_core),
        permute_blk(jnp.concatenate([near, near_x]), to_core),
        permute_blk(far, to_x),
    )
    return together(
        *forward(3, *begun, near_core, far_x, far_core), permute_blk(far_x, to_core)
    )


def scatter_terms(give_far, give_near, keep_far, keep_near, grad):
    def send(move, *values):
        sizes = [value.size // OWN for value in values]
        message = [value.astype(f16).reshape(-1, OWN) for value in values]
        got = permute_blk(jnp.concatenate(message) if len(message) > 1 else message[0], move)
        got = got.astype(f32)
        starts = [sum(sizes[:i]) for i in range(len(sizes))]
        return [
            got[at : at + size].reshape(value.shape)
            for at, size, value in zip(starts, sizes, values)
        ]

    def rounded(value):
        return value.astype(f16).astype(f32)

    far, more = send(to_core, give_far, grad)
    far, grad = keep_far + far, rounded(rounded(grad) + more)
    far_x, more = send(to_x, far[:3], grad)
    far, grad = far[3:] + far_x, rounded(grad + more)
    (near,) = send(to_core, give_near)
    near = keep_near + near
    (near_x,) = send(to_x, near[:5])
    passed, grad_2 = send(to_z_by_core(2), far, grad)
    near = near[5:] + near_x
    two = jnp.concatenate([near[:1] + passed[:1], near[1:2]])
    got_2, grad_4 = send(to_z_by_core(2), two, grad_2)
    got_1, grad_1, grad_3 = send(to_z_by_core(1), near[2:4] + passed[1:], grad, grad_2)
    got = got_2 + got_1
    mine = jnp.stack([grad_1, grad_2, grad_3, grad_4])
    other, theirs = send(to_core, got[1], mine)
    return near[4] + got[0] + other, grad, mine, theirs


def per_device(
    node_features,
    weight_matrix,
    bias_vector,
    node_degree,
    tile_values,
    tile_row,
    tile_count,
    cotangent,
):
    n_out = weight_matrix.shape[1]
    tiles = tile_values.reshape(-1, SLOTS * TILE, TILE)
    rows = tile_row.reshape(-1)
    count = tile_count.reshape(-1)
    degree = node_degree.reshape(OWN // TILE, TILE)
    place = lax.axis_index("blk").astype(jnp.int32).reshape(1)

    own = call(
        scale_kernel,
        shape((2, BLOCK, TILE), bf16),
        [HBM] * 3,
        [
            pltpu.VMEM((OWN, TILE), bf16),
            pltpu.VMEM((OWN // TILE, TILE), jnp.int32),
            pltpu.VMEM((OWN, n_out), bf16),
            pltpu.SemaphoreType.DMA((3,)),
        ],
    )(node_features, degree, cotangent)
    acc = shape(((ROW_TILES + 1) * TILE, TILE), f32)
    marks = shape((BLOCK - OWN, TILE), f32)

    smem = (after(rows, own), after(count, own))

    def products(kernel, outs, scratch, *pieces):
        ins = [SMEM] * 3 + [VMEM] * (1 + len(pieces))
        return call(kernel, outs, ins, scratch, 1 << 29)(place, *smem, tiles, *pieces)

    def forward(step, *pieces):
        kernel = functools.partial(forward_kernel, FORWARD_ORDERS[step])
        return products(kernel, (acc, marks), [], *pieces)

    partial = products(
        forward_last_kernel,
        shape((8, BLOCK, TILE), f32),
        [pltpu.VMEM(acc.shape, f32)],
        *gather_blocks(own, forward),
    )
    parts = lax.all_to_all(partial.astype(f16), "rep", 0, 0).astype(f32)
    hidden, back, grad, factor = call(
        middle_kernel,
        (
            shape((OWN, n_out), bf16),
            shape((TILE, OWN), f32),
            shape((8, 32, 256), f32),
            shape((2, 8, TILE), f32),
        ),
        [VMEM] * 6,
        cost=1 << 27,
    )(parts, weight_matrix, bias_vector.reshape(1, -1), degree, node_features, cotangent)

    sent = jnp.concatenate([jnp.broadcast_to(back[None], (8, TILE, OWN)), grad], 1).astype(f16)
    got = lax.all_to_all(sent, "rep", 0, 0).astype(f32)
    got_back = got[:, :TILE]

    orders = (GIVE_FAR, GIVE_NEAR, KEEP_FAR, KEEP_NEAR)
    terms = products(
        functools.partial(backward_kernel, orders),
        tuple(shape((len(order), TILE, OWN), f32) for order in orders),
        [pltpu.VMEM((ROW_TILES + 1, 2 * TILE, TILE), bf16)],
        got_back,
    )
    total, *grads = scatter_terms(*terms, jnp.sum(got[:, TILE:], 0))
    row_scale = 1.0 / jnp.sqrt(node_degree.astype(f32))
    input_grad = ((total * row_scale[None, :]).T * factor[0, :1, :]).astype(bf16)

    grad = call(sum_kernel, shape((32, 256), f32), [SMEM] + [VMEM] * 3)(place, *grads)
    grad = jnp.broadcast_to(grad.astype(f16)[None], (8, 32, 256))
    slices = lax.all_to_all(grad, "rep", 0, 0).astype(f32)
    weight_grad = call(assemble_kernel, shape((TILE, n_out), f32), [VMEM] * 2)(slices, factor)
    return hidden, weight_grad, input_grad


def solution(mesh):
    in_specs = (
        P(("blk", "rep"), None),
        P(),
        P(),
        P(("blk", "rep")),
        P("blk", "rep", None, None, None, None),
        P("blk", "rep", None, None),
        P("blk", "rep", None),
        P(("blk", "rep"), None),
    )
    out_specs = (P(("blk", "rep"), None), P(), P(("blk", "rep"), None))
    return jax.shard_map(
        per_device, mesh=mesh, in_specs=in_specs, out_specs=out_specs, check_vma=False
    )
```

```python
import functools

import jax
import jax.numpy as jnp
from jax import lax
from jax.experimental import pallas as pl
from jax.experimental.pallas import tpu as pltpu
from jax.sharding import PartitionSpec as P

f32, bf16, f16 = jnp.float32, jnp.bfloat16, jnp.float16

TILE = 128
OWN = 256
BLOCK = OWN + 16
N_X, N_Z, N_C = 2, 8, 2
N_Y = 4
SLOTS = 2
ROW_TILES = 16
VMEM_LIMIT = 16 * 1024 * 1024


def blk_index(x, z, c):
    return (x * N_Z + z) * N_C + c


def permute_blk(value, move):
    pairs = []
    for x in range(N_X):
        for z in range(N_Z):
            for c in range(N_C):
                pairs.append((blk_index(x, z, c), blk_index(*move(x, z, c))))
    return lax.ppermute(value, "blk", pairs)


def to_core(x, z, c):
    return x, z, 1 - c


def to_x(x, z, c):
    return 1 - x, z, c


def to_z_xor(bits, other_x=0):
    return lambda x, z, c: (x ^ other_x, z ^ bits, c)


def to_z_by_core(distance):
    return lambda x, z, c: (x, (z + (distance if c == 0 else -distance)) % N_Z, c)


def exponent_above(largest):
    return jnp.ceil(jnp.log2(jnp.maximum(largest, 1e-30))) + 1.0


def as_column(row):
    n = row.shape[1]
    diagonal = lax.broadcasted_iota(jnp.int32, (n, n), 0) == lax.broadcasted_iota(
        jnp.int32, (n, n), 1
    )
    return jnp.sum(jnp.where(diagonal, row, 0.0), axis=1, keepdims=True)


def scale_of(degree):
    scale = 1.0 / jnp.sqrt(degree.astype(f32))
    rows = [scale[i : i + 1, :] for i in range(scale.shape[0])]
    return jnp.concatenate(rows, 1), jnp.concatenate([as_column(r) for r in rows], 0)


def split(value):
    high = value.astype(bf16)
    return high, (value - high.astype(f32)).astype(bf16)


def scale_kernel(features_hbm, degree_hbm, cot_hbm, own_ref, features_ref, degree_ref, cot_ref, sems):
    copies = [
        pltpu.make_async_copy(src, dst, sems.at[i])
        for i, (src, dst) in enumerate(
            [(degree_hbm, degree_ref), (features_hbm, features_ref), (cot_hbm, cot_ref)]
        )
    ]
    for copy in copies:
        copy.start()
    copies[0].wait()
    _, column = scale_of(degree_ref[...])
    copies[1].wait()
    scaled = (features_ref[...].astype(f32) * column).astype(bf16)
    own_ref[0, :OWN, :] = scaled
    copies[2].wait()
    cot = jnp.max(jnp.abs(cot_ref[...].astype(f32)))
    feature = jnp.max(jnp.abs(scaled.astype(f32)))
    rows = lax.broadcasted_iota(jnp.int32, (BLOCK - OWN, TILE), 0)
    own_ref[0, OWN:, :] = jnp.where(rows < 8, cot, feature).astype(bf16)
    own_ref[1] = own_ref[0]


def column_block(at, dx, dz, dc):
    x, z, c = at // (N_Z * N_C), at // N_C % N_Z, at % N_C
    z = (z + N_Z + (1 - 2 * c) * dz) % N_Z
    return blk_index(x + dx - 2 * dx * x, z, c + dc - 2 * dc * c)


def add_products(order, place_ref, rows_ref, count_ref, tiles_ref, pieces, acc_ref):
    column_blocks = [
        column_block(place_ref[0], *block) for blocks in order for block in blocks
    ]
    refs = [(ref, at) for ref, blocks in zip(pieces, order, strict=True) for at in range(len(blocks))]
    largest = None
    for i, (ref, at) in enumerate(refs):
        marks = ref[at, OWN:, :].astype(f32)
        largest = marks if largest is None else jnp.maximum(largest, marks)
        for half in range(OWN // TILE):
            k = column_blocks[i] * (OWN // TILE) + half
            part = ref[at, half * TILE : (half + 1) * TILE, :]
            product = jnp.dot(tiles_ref[k], part, preferred_element_type=f32)
            for slot in range(SLOTS):
                row = rows_ref[k * SLOTS + slot]
                row = jnp.where(slot < count_ref[k], row, ROW_TILES)
                where = pl.ds(pl.multiple_of(row * TILE, TILE), TILE)
                acc_ref[where, :] += product[slot * TILE : (slot + 1) * TILE, :]
    return largest


def forward_kernel(order, place_ref, rows_ref, count_ref, tiles_ref, *refs):
    (acc_ref, marks_ref), refs = refs[-2:], refs[:-2]
    pieces = refs[-len(order) :]
    if len(refs) > len(order):
        acc_ref[...] = refs[0][...]
    else:
        acc_ref[...] = jnp.zeros_like(acc_ref)
    marks = add_products(order, place_ref, rows_ref, count_ref, tiles_ref, pieces, acc_ref)
    if len(refs) > len(order):
        marks = jnp.maximum(marks, refs[1][...])
    marks_ref[...] = marks


def forward_last_kernel(place_ref, rows_ref, count_ref, tiles_ref, begun_ref, begun_marks, *refs):
    pieces, (out_ref, acc_ref) = refs[:-2], refs[-2:]
    acc_ref[...] = begun_ref[...]
    largest = add_products(
        LAST_ORDER, place_ref, rows_ref, count_ref, tiles_ref, pieces, acc_ref
    )
    marks = exponent_above(jnp.maximum(largest, begun_marks[...]))
    shrink = 2.0 * jnp.exp2(-marks[8:9, :])
    for r in range(out_ref.shape[0]):
        out_ref[r, :OWN, :] = acc_ref[r * OWN : (r + 1) * OWN, :] * shrink
        out_ref[r, OWN:, :] = marks


FORWARD_ORDERS = [
    [[(0, 0, 0), (0, 0, 1)]],
    [[(1, 0, 0), (1, 0, 1)], [(0, -1, 0), (0, -1, 1), (0, -2, 0), (0, -2, 1)]],
    [[(1, -1, 0), (1, -1, 1), (1, -2, 0), (1, -2, 1)], [(0, -3, 0), (0, -3, 1), (0, 4, 0)]],
    [
        [(dx, i, dc) for dx in (0, 1) for i in (1, 2) for dc in (1, 0)],
        [(0, 3, 1), (0, 3, 0), (0, 4, 1)],
    ],
    [[(1, -3, 0), (1, -3, 1), (1, 4, 0)]],
]
LAST_ORDER = [[(1, 3, 1), (1, 3, 0), (1, 4, 1)]]


def middle_kernel(
    parts_ref,
    weight_ref,
    bias_ref,
    degree_ref,
    features_ref,
    cot_ref,
    hidden_ref,
    back_ref,
    grad_ref,
    factor_ref,
):
    row_scale, column_scale = scale_of(degree_ref[...])
    summed = jnp.zeros((OWN, TILE), f32)
    cot_mark = feature_mark = None
    for r in range(parts_ref.shape[0]):
        cot_r, feature_r = parts_ref[r, OWN : OWN + 1, :], parts_ref[r, OWN + 8 : OWN + 9, :]
        summed += parts_ref[r, :OWN, :] * (0.5 * jnp.exp2(feature_r))
        cot_mark = cot_r if cot_mark is None else jnp.maximum(cot_mark, cot_r)
        feature_mark = feature_r if feature_mark is None else jnp.maximum(feature_mark, feature_r)
    weight = weight_ref[...]
    high, low = split(summed)
    mixed = jnp.dot(high, weight, preferred_element_type=f32)
    mixed += jnp.dot(low, weight, preferred_element_type=f32)
    pre = column_scale * mixed + bias_ref[...]
    root = 0.7978845608028654
    square = pre * pre
    bent = jnp.tanh(root * pre * (1.0 + 0.044715 * square))
    half_up = 0.5 * (1.0 + bent)
    hidden_ref[...] = (pre * half_up).astype(bf16)
    slope = half_up + 0.5 * pre * (1.0 - bent * bent) * (root * (1.0 + 0.134145 * square))
    shrink = jnp.exp2(-cot_mark[:, :1])
    grad = cot_ref[...].astype(f32) * shrink * slope
    high, low = split(grad)
    across = (((1,), (1,)), ((), ()))
    back = lax.dot_general(weight, high, across, preferred_element_type=f32)
    back += lax.dot_general(weight, low, across, preferred_element_type=f32)
    weight_mark = exponent_above(jnp.max(jnp.abs(weight.astype(f32)), axis=(0, 1), keepdims=True))
    back_ref[...] = back * row_scale * (64.0 * jnp.exp2(-weight_mark))
    down = (((0,), (0,)), ((), ()))
    features = features_ref[...]
    local = lax.dot_general(features, high, down, preferred_element_type=f32)
    local += lax.dot_general(features, low, down, preferred_element_type=f32)
    local = local * (0.25 * jnp.exp2(-feature_mark[:, :1]))
    for r in range(grad_ref.shape[0]):
        i, j = r // 2, r % 2
        grad_ref[r] = local[i * 32 : (i + 1) * 32, j * 256 : (j + 1) * 256]
    one = jnp.ones((8, TILE), f32)
    factor_ref[0] = one * (16.0 * jnp.exp2(cot_mark + weight_mark))
    factor_ref[1] = one * (jnp.exp2(cot_mark + feature_mark) / 64.0)


def backward_kernel(orders, place_ref, rows_ref, count_ref, tiles_ref, back_ref, *refs):
    outs, group_ref = refs[:-1], refs[-1]
    for r in range(ROW_TILES):
        value = back_ref[r // 2, :, (r % 2) * TILE : (r % 2 + 1) * TILE] * (1.0 / 1024.0)
        high, low = split(value)
        group_ref[r, :TILE, :] = high
        group_ref[r, TILE:, :] = low
    group_ref[ROW_TILES] = jnp.zeros(group_ref.shape[1:], bf16)
    for ref, order in zip(outs, orders, strict=True):
        for at, block in enumerate(order):
            block = column_block(place_ref[0], *block)
            for half in range(OWN // TILE):
                k = block * (OWN // TILE) + half
                picked = []
                for slot in range(SLOTS):
                    row = rows_ref[k * SLOTS + slot]
                    picked.append(group_ref[jnp.where(slot < count_ref[k], row, ROW_TILES)])
                both = jnp.dot(
                    jnp.concatenate(picked, 1), tiles_ref[k], preferred_element_type=f32
                )
                ref[at, :, half * TILE : (half + 1) * TILE] = both[:TILE] + both[TILE:]


def join_kernel(first_ref, second_ref, _, out_ref):
    n = first_ref.shape[0]
    out_ref[:n] = first_ref[...]
    out_ref[n:] = second_ref[...]


def copy_kernel(value_ref, *refs):
    refs[-1][...] = value_ref[...]


def finish_kernel(mine_ref, theirs_ref, degree_ref, factor_ref, slices_ref, input_ref, weight_ref):
    factor = jnp.concatenate([factor_ref[1, :1, :]] * 2, 1)
    for r in range(slices_ref.shape[0]):
        i, j = r // 2, r % 2
        weight_ref[i * 32 : (i + 1) * 32, j * 256 : (j + 1) * 256] = slices_ref[r] * factor
    _, column_scale = scale_of(degree_ref[...])
    total = (mine_ref[...] + theirs_ref[...]).T
    input_ref[...] = (column_scale * total * factor_ref[0, :1, :]).astype(bf16)


GIVE_FAR = [(dx, *rest) for dx in (1, 0) for rest in ((4, 1), (-3, 1), (-3, 0))]
GIVE_NEAR = [(dx, *rest) for dx in (1, 0) for rest in ((-2, 1), (-2, 0), (-1, 1), (-1, 0), (0, 1))]
KEEP_FAR = [(dx, *rest) for dx in (1, 0) for rest in ((4, 0), (3, 0), (3, 1))]
KEEP_NEAR = [(dx, *rest) for dx in (1, 0) for rest in ((2, 0), (2, 1), (1, 0), (1, 1), (0, 0))]


SMEM = pl.BlockSpec(memory_space=pltpu.SMEM)
VMEM = pl.BlockSpec(memory_space=pltpu.VMEM)
HBM = pl.BlockSpec(memory_space=pltpu.HBM)


def shape(dims, dtype):
    return jax.ShapeDtypeStruct(dims, dtype)


def call(kernel, outs, ins, scratch=(), cost=0):
    return pl.pallas_call(
        kernel,
        out_shape=outs,
        in_specs=ins,
        out_specs=jax.tree.map(lambda _: VMEM, outs),
        scratch_shapes=list(scratch),
        compiler_params=pltpu.CompilerParams(vmem_limit_bytes=VMEM_LIMIT),
        cost_estimate=pl.CostEstimate(flops=cost, bytes_accessed=1 << 20, transcendentals=0),
    )


def after(value, *others):
    return lax.optimization_barrier((value, *others))[0]


def together(*values):
    return lax.optimization_barrier(values)


def gather_blocks(own, forward):
    pair = lax.dynamic_update_slice(own, permute_blk(own[:1], to_core), (1, 0, 0))
    *begun, pair_x, near_1, near_2 = together(
        *forward(0, pair),
        permute_blk(pair, to_x),
        permute_blk(pair, to_z_by_core(1)),
        permute_blk(pair, to_z_by_core(2)),
    )
    near = jnp.concatenate([near_1, near_2])
    *begun, far, near_x = together(
        *forward(1, *begun, pair_x, near),
        permute_blk(near[:3], to_z_by_core(2)),
        permute_blk(near, to_x),
    )
    far_x = permute_blk(far, to_x)
    all_near = call(join_kernel, shape((8, BLOCK, TILE), bf16), [VMEM] * 3, cost=1 << 31)(
        near, near_x, far
    )
    *begun, far_core, near_core = together(
        *forward(2, *begun, near_x, far),
        permute_blk(far, to_core),
        permute_blk(all_near, to_core),
    )
    *begun, far_x = together(*forward(3, *begun, near_core, far_core), far_x)
    return together(*forward(4, *begun, far_x), permute_blk(far_x, to_core))


def behind(value, *others):
    corners = [other.reshape(-1, OWN)[:16, :TILE].astype(f32) for other in others]
    ins = [VMEM] * (1 + len(others))
    return call(copy_kernel, shape(value.shape, value.dtype), ins, cost=1 << 31)(value, *corners)


def scatter_terms(backward, grad):
    def rounded(value):
        return value.astype(f16).astype(f32)

    def with_grad(terms, grad):
        return jnp.concatenate([terms.reshape(-1, OWN), grad]).astype(f16)

    def parted(got, terms):
        n = terms.shape[0] * TILE
        got = got.astype(f32)
        return got[:n].reshape(terms.shape), got[n:]

    give_far, keep_far = backward(GIVE_FAR, KEEP_FAR)
    far, more = parted(permute_blk(with_grad(give_far, grad), to_core), give_far)
    give_near, keep_near = backward(GIVE_NEAR, KEEP_NEAR)
    far, grad = keep_far + far, rounded(rounded(grad) + more)
    out = after(with_grad(far[:3], grad))
    mine = behind(grad, out).astype(f16)
    fan = [permute_blk(mine, to_z_xor(1, other_x)).astype(f32) for other_x in (0, 1)]
    far_x, more = parted(permute_blk(out, to_x), far[:3])
    near = keep_near + permute_blk(give_near.astype(f16), to_core).astype(f32)
    far = far[3:] + far_x
    grad = rounded((grad + more) + (fan[0] + fan[1]))
    out = after(with_grad(far, grad))
    near_out = after(near[:5].astype(f16))
    mine = behind(grad, out, near_out).astype(f16)
    grad = grad + permute_blk(mine, to_z_xor(4)).astype(f32)
    near_x = permute_blk(near_out, to_x).astype(f32)
    out = permute_blk(out, to_z_by_core(2))
    passed, more = parted(out, far)
    grad = grad + (more + permute_blk(out[-32:], to_core).astype(f32))
    near = near[5:] + near_x
    two = jnp.concatenate([near[:1] + passed[:1], near[1:2]]).astype(f16)
    two, one = together(two, (near[2:4] + passed[1:]).astype(f16))
    grad = after(jnp.broadcast_to(grad.astype(f16)[None], (8, 32, 256)), two, one)
    got = permute_blk(two, to_z_by_core(2)).astype(f32) + permute_blk(one, to_z_by_core(1)).astype(f32)
    return near[4] + got[0], permute_blk(got[1].astype(f16), to_core).astype(f32), grad


def per_device(
    node_features,
    weight_matrix,
    bias_vector,
    node_degree,
    tile_values,
    tile_row,
    tile_count,
    cotangent,
):
    n_out = weight_matrix.shape[1]
    tiles = tile_values.reshape(-1, SLOTS * TILE, TILE)
    rows = tile_row.reshape(-1)
    count = tile_count.reshape(-1)
    degree = node_degree.reshape(OWN // TILE, TILE)
    place = lax.axis_index("blk").astype(jnp.int32).reshape(1)

    own = call(
        scale_kernel,
        shape((2, BLOCK, TILE), bf16),
        [HBM] * 3,
        [
            pltpu.VMEM((OWN, TILE), bf16),
            pltpu.VMEM((OWN // TILE, TILE), jnp.int32),
            pltpu.VMEM((OWN, n_out), bf16),
            pltpu.SemaphoreType.DMA((3,)),
        ],
    )(node_features, degree, cotangent)
    acc = shape(((ROW_TILES + 1) * TILE, TILE), f32)
    marks = shape((BLOCK - OWN, TILE), f32)

    smem = (after(rows, own), after(count, own))

    def products(kernel, outs, scratch, *pieces):
        ins = [SMEM] * 3 + [VMEM] * (1 + len(pieces))
        return call(kernel, outs, ins, scratch, 1 << 29)(place, *smem, tiles, *pieces)

    def forward(step, *pieces):
        kernel = functools.partial(forward_kernel, FORWARD_ORDERS[step])
        return products(kernel, (acc, marks), [], *pieces)

    partial = products(
        forward_last_kernel,
        shape((8, BLOCK, TILE), f32),
        [pltpu.VMEM(acc.shape, f32)],
        *gather_blocks(own, forward),
    )
    parts = lax.all_to_all(partial.astype(f16), "rep", 0, 0).astype(f32)
    hidden, back, grad, factor = call(
        middle_kernel,
        (
            shape((OWN, n_out), bf16),
            shape((TILE, OWN), f32),
            shape((8, 32, 256), f32),
            shape((2, 8, TILE), f32),
        ),
        [VMEM] * 6,
        cost=1 << 27,
    )(parts, weight_matrix, bias_vector.reshape(1, -1), degree, node_features, cotangent)

    sent = jnp.concatenate([jnp.broadcast_to(back[None], (8, TILE, OWN)), grad], 1).astype(f16)
    got = lax.all_to_all(sent, "rep", 0, 0).astype(f32)
    got_back = got[:, :TILE]

    def backward(*orders):
        return products(
            functools.partial(backward_kernel, orders),
            tuple(shape((len(order), TILE, OWN), f32) for order in orders),
            [pltpu.VMEM((ROW_TILES + 1, 2 * TILE, TILE), bf16)],
            got_back,
        )

    *halves, grad = scatter_terms(backward, jnp.sum(got[:, TILE:], 0))
    slices = lax.all_to_all(grad, "rep", 0, 0).astype(f32)
    input_grad, weight_grad = call(
        finish_kernel, (shape((OWN, TILE), bf16), shape((TILE, n_out), f32)), [VMEM] * 5
    )(*halves, degree, factor, slices)
    return hidden, weight_grad, input_grad


def solution(mesh):
    in_specs = (
        P(("blk", "rep"), None),
        P(),
        P(),
        P(("blk", "rep")),
        P("blk", "rep", None, None, None, None),
        P("blk", "rep", None, None),
        P("blk", "rep", None),
        P(("blk", "rep"), None),
    )
    out_specs = (P(("blk", "rep"), None), P(), P(("blk", "rep"), None))
    return jax.shard_map(
        per_device, mesh=mesh, in_specs=in_specs, out_specs=out_specs, check_vma=False
    )
```

```python
import functools

import jax
import jax.numpy as jnp
from jax import lax
from jax.experimental import pallas as pl
from jax.experimental.pallas import tpu as pltpu
from jax.sharding import PartitionSpec as P

f32, bf16, f16 = jnp.float32, jnp.bfloat16, jnp.float16

TILE = 128
OWN = 256
BLOCK = OWN + 16
N_X, N_Z, N_C = 2, 8, 2
N_Y = 4
SLOTS = 2
ROW_TILES = 16
VMEM_LIMIT = 16 * 1024 * 1024


def blk_index(x, z, c):
    return (x * N_Z + z) * N_C + c


def permute_blk(value, move):
    pairs = []
    for x in range(N_X):
        for z in range(N_Z):
            for c in range(N_C):
                pairs.append((blk_index(x, z, c), blk_index(*move(x, z, c))))
    return lax.ppermute(value, "blk", pairs)


def to_core(x, z, c):
    return x, z, 1 - c


def to_x(x, z, c):
    return 1 - x, z, c


def to_z_xor(bits, other_x=0):
    return lambda x, z, c: (x ^ other_x, z ^ bits, c)


def to_z_by_core(distance):
    return lambda x, z, c: (x, (z + (distance if c == 0 else -distance)) % N_Z, c)


def exponent_above(largest):
    return jnp.ceil(jnp.log2(jnp.maximum(largest, 1e-30))) + 1.0


def as_column(row):
    n = row.shape[1]
    diagonal = lax.broadcasted_iota(jnp.int32, (n, n), 0) == lax.broadcasted_iota(
        jnp.int32, (n, n), 1
    )
    return jnp.sum(jnp.where(diagonal, row, 0.0), axis=1, keepdims=True)


def scale_of(degree):
    scale = 1.0 / jnp.sqrt(degree.astype(f32))
    rows = [scale[i : i + 1, :] for i in range(scale.shape[0])]
    return jnp.concatenate(rows, 1), jnp.concatenate([as_column(r) for r in rows], 0)


def split(value):
    high = value.astype(bf16)
    return high, (value - high.astype(f32)).astype(bf16)


def scale_kernel(
    features_hbm, degree_hbm, cot_hbm, own_ref, pair_ref, features_ref, degree_ref, cot_ref, sems
):
    copies = [
        pltpu.make_async_copy(src, dst, sems.at[i])
        for i, (src, dst) in enumerate(
            [(degree_hbm, degree_ref), (features_hbm, features_ref), (cot_hbm, cot_ref)]
        )
    ]
    for copy in copies:
        copy.start()
    copies[0].wait()
    _, column = scale_of(degree_ref[...])
    copies[1].wait()
    scaled = (features_ref[...].astype(f32) * column).astype(bf16)
    own_ref[0, :OWN, :] = scaled
    copies[2].wait()
    cot = jnp.max(jnp.abs(cot_ref[...].astype(f32)))
    feature = jnp.max(jnp.abs(scaled.astype(f32)))
    rows = lax.broadcasted_iota(jnp.int32, (BLOCK - OWN, TILE), 0)
    own_ref[0, OWN:, :] = jnp.where(rows < 8, cot, feature).astype(bf16)
    pair_ref[0] = own_ref[0]
    pair_ref[1] = own_ref[0]


def column_block(at, dx, dz, dc):
    x, z, c = at // (N_Z * N_C), at // N_C % N_Z, at % N_C
    z = (z + N_Z + (1 - 2 * c) * dz) % N_Z
    return blk_index(x + dx - 2 * dx * x, z, c + dc - 2 * dc * c)


def add_products(order, place_ref, rows_ref, count_ref, tiles_ref, pieces, acc_ref):
    column_blocks = [
        column_block(place_ref[0], *block) for blocks in order for block in blocks
    ]
    refs = [(ref, at) for ref, blocks in zip(pieces, order, strict=True) for at in range(len(blocks))]
    largest = None
    for i, (ref, at) in enumerate(refs):
        marks = ref[at, OWN:, :].astype(f32)
        largest = marks if largest is None else jnp.maximum(largest, marks)
        for half in range(OWN // TILE):
            k = column_blocks[i] * (OWN // TILE) + half
            part = ref[at, half * TILE : (half + 1) * TILE, :]
            product = jnp.dot(tiles_ref[k], part, preferred_element_type=f32)
            for slot in range(SLOTS):
                row = rows_ref[k * SLOTS + slot]
                row = jnp.where(slot < count_ref[k], row, ROW_TILES)
                where = pl.ds(pl.multiple_of(row * TILE, TILE), TILE)
                acc_ref[where, :] += product[slot * TILE : (slot + 1) * TILE, :]
    return largest


def forward_kernel(order, place_ref, rows_ref, count_ref, tiles_ref, *refs):
    (acc_ref, marks_ref), refs = refs[-2:], refs[:-2]
    pieces = refs[-len(order) :]
    if len(refs) > len(order):
        acc_ref[...] = refs[0][...]
    else:
        acc_ref[...] = jnp.zeros_like(acc_ref)
    marks = add_products(order, place_ref, rows_ref, count_ref, tiles_ref, pieces, acc_ref)
    if len(refs) > len(order):
        marks = jnp.maximum(marks, refs[1][...])
    marks_ref[...] = marks


def forward_last_kernel(place_ref, rows_ref, count_ref, tiles_ref, begun_ref, begun_marks, *refs):
    pieces, (out_ref, acc_ref) = refs[:-2], refs[-2:]
    acc_ref[...] = begun_ref[...]
    largest = add_products(
        LAST_ORDER, place_ref, rows_ref, count_ref, tiles_ref, pieces, acc_ref
    )
    marks = exponent_above(jnp.maximum(largest, begun_marks[...]))
    shrink = 2.0 * jnp.exp2(-marks[8:9, :])
    for r in range(out_ref.shape[0]):
        out_ref[r, :OWN, :] = acc_ref[r * OWN : (r + 1) * OWN, :] * shrink
        out_ref[r, OWN:, :] = marks


FORWARD_ORDERS = [
    [[(0, 0, 0), (0, 0, 1)]],
    [[(1, 0, 0), (1, 0, 1)], [(0, -1, 0), (0, -1, 1), (0, -2, 0), (0, -2, 1)]],
    [[(1, -1, 0), (1, -1, 1), (1, -2, 0), (1, -2, 1)], [(0, -3, 0), (0, -3, 1), (0, 4, 0)]],
    [
        [(dx, i, dc) for dx in (0, 1) for i in (1, 2) for dc in (1, 0)],
        [(0, 3, 1), (0, 3, 0), (0, 4, 1)],
    ],
    [[(1, -3, 0), (1, -3, 1), (1, 4, 0)]],
]
LAST_ORDER = [[(1, 3, 1), (1, 3, 0), (1, 4, 1)]]


def middle_kernel(
    parts_ref,
    weight_ref,
    bias_ref,
    degree_ref,
    features_ref,
    cot_ref,
    hidden_ref,
    back_ref,
    grad_ref,
    factor_ref,
):
    row_scale, column_scale = scale_of(degree_ref[...])
    summed = jnp.zeros((OWN, TILE), f32)
    cot_mark = feature_mark = None
    for r in range(parts_ref.shape[0]):
        cot_r, feature_r = parts_ref[r, OWN : OWN + 1, :], parts_ref[r, OWN + 8 : OWN + 9, :]
        summed += parts_ref[r, :OWN, :] * (0.5 * jnp.exp2(feature_r))
        cot_mark = cot_r if cot_mark is None else jnp.maximum(cot_mark, cot_r)
        feature_mark = feature_r if feature_mark is None else jnp.maximum(feature_mark, feature_r)
    weight = weight_ref[...]
    high, low = split(summed)
    mixed = jnp.dot(high, weight, preferred_element_type=f32)
    mixed += jnp.dot(low, weight, preferred_element_type=f32)
    pre = column_scale * mixed + bias_ref[...]
    root = 0.7978845608028654
    square = pre * pre
    bent = jnp.tanh(root * pre * (1.0 + 0.044715 * square))
    half_up = 0.5 * (1.0 + bent)
    hidden_ref[...] = (pre * half_up).astype(bf16)
    slope = half_up + 0.5 * pre * (1.0 - bent * bent) * (root * (1.0 + 0.134145 * square))
    shrink = jnp.exp2(-cot_mark[:, :1])
    grad = cot_ref[...].astype(f32) * shrink * slope
    high, low = split(grad)
    across = (((1,), (1,)), ((), ()))
    back = lax.dot_general(weight, high, across, preferred_element_type=f32)
    back += lax.dot_general(weight, low, across, preferred_element_type=f32)
    weight_mark = exponent_above(jnp.max(jnp.abs(weight.astype(f32)), axis=(0, 1), keepdims=True))
    back_ref[...] = back * row_scale * (64.0 * jnp.exp2(-weight_mark))
    down = (((0,), (0,)), ((), ()))
    features = features_ref[...]
    local = lax.dot_general(features, high, down, preferred_element_type=f32)
    local += lax.dot_general(features, low, down, preferred_element_type=f32)
    local = local * (0.25 * jnp.exp2(-feature_mark[:, :1]))
    for r in range(grad_ref.shape[0]):
        i, j = r // 2, r % 2
        grad_ref[r] = local[i * 32 : (i + 1) * 32, j * 256 : (j + 1) * 256]
    one = jnp.ones((8, TILE), f32)
    factor_ref[0] = one * (16.0 * jnp.exp2(cot_mark + weight_mark))
    factor_ref[1] = one * (jnp.exp2(cot_mark + feature_mark) / 64.0)


def backward_kernel(orders, place_ref, rows_ref, count_ref, tiles_ref, back_ref, *refs):
    outs, group_ref = refs[:-1], refs[-1]
    for r in range(ROW_TILES):
        value = back_ref[r // 2, :, (r % 2) * TILE : (r % 2 + 1) * TILE] * (1.0 / 1024.0)
        high, low = split(value)
        group_ref[r, :TILE, :] = high
        group_ref[r, TILE:, :] = low
    group_ref[ROW_TILES] = jnp.zeros(group_ref.shape[1:], bf16)
    for ref, order in zip(outs, orders, strict=True):
        for at, block in enumerate(order):
            block = column_block(place_ref[0], *block)
            for half in range(OWN // TILE):
                k = block * (OWN // TILE) + half
                picked = []
                for slot in range(SLOTS):
                    row = rows_ref[k * SLOTS + slot]
                    picked.append(group_ref[jnp.where(slot < count_ref[k], row, ROW_TILES)])
                both = jnp.dot(
                    jnp.concatenate(picked, 1), tiles_ref[k], preferred_element_type=f32
                )
                ref[at, :, half * TILE : (half + 1) * TILE] = both[:TILE] + both[TILE:]


def join_kernel(first_ref, second_ref, _, out_ref):
    n = first_ref.shape[0]
    out_ref[:n] = first_ref[...]
    out_ref[n:] = second_ref[...]


def copy_kernel(value_ref, *refs):
    refs[-1][...] = value_ref[...]


def finish_kernel(mine_ref, theirs_ref, degree_ref, factor_ref, slices_ref, input_ref, weight_ref):
    factor = jnp.concatenate([factor_ref[1, :1, :]] * 2, 1)
    for r in range(slices_ref.shape[0]):
        i, j = r // 2, r % 2
        weight_ref[i * 32 : (i + 1) * 32, j * 256 : (j + 1) * 256] = slices_ref[r] * factor
    _, column_scale = scale_of(degree_ref[...])
    total = (mine_ref[...] + theirs_ref[...]).T
    input_ref[...] = (column_scale * total * factor_ref[0, :1, :]).astype(bf16)


GIVE_FAR = [(dx, *rest) for dx in (1, 0) for rest in ((4, 1), (-3, 1), (-3, 0))]
GIVE_NEAR = [(dx, *rest) for dx in (1, 0) for rest in ((-2, 1), (-2, 0), (-1, 1), (-1, 0), (0, 1))]
KEEP_FAR = [(dx, *rest) for dx in (1, 0) for rest in ((4, 0), (3, 0), (3, 1))]
KEEP_NEAR = [(dx, *rest) for dx in (1, 0) for rest in ((2, 0), (2, 1), (1, 0), (1, 1), (0, 0))]


SMEM = pl.BlockSpec(memory_space=pltpu.SMEM)
VMEM = pl.BlockSpec(memory_space=pltpu.VMEM)
HBM = pl.BlockSpec(memory_space=pltpu.HBM)


def shape(dims, dtype):
    return jax.ShapeDtypeStruct(dims, dtype)


def call(kernel, outs, ins, scratch=(), cost=0, limit=VMEM_LIMIT):
    return pl.pallas_call(
        kernel,
        out_shape=outs,
        in_specs=ins,
        out_specs=jax.tree.map(lambda _: VMEM, outs),
        scratch_shapes=list(scratch),
        compiler_params=pltpu.CompilerParams(vmem_limit_bytes=limit),
        cost_estimate=pl.CostEstimate(flops=cost, bytes_accessed=1 << 20, transcendentals=0),
    )


def after(value, *others):
    return lax.optimization_barrier((value, *others))[0]


def together(*values):
    return lax.optimization_barrier(values)


def gather_blocks(own, pair, forward):
    pair = lax.dynamic_update_slice(pair, permute_blk(own, to_core), (1, 0, 0))
    *begun, near_2, near_1, pair_x = together(
        *forward(0, pair),
        permute_blk(pair, to_z_by_core(2)),
        permute_blk(pair, to_z_by_core(1)),
        permute_blk(pair, to_x),
    )
    near = jnp.concatenate([near_1, near_2])
    *begun, far, near_x = together(
        *forward(1, *begun, pair_x, near),
        permute_blk(near[:3], to_z_by_core(2)),
        permute_blk(near, to_x),
    )
    far_x = permute_blk(far, to_x)
    all_near = call(join_kernel, shape((8, BLOCK, TILE), bf16), [VMEM] * 3, cost=1 << 31)(
        near, near_x, far
    )
    *begun, far_core, near_core = together(
        *forward(2, *begun, near_x, far),
        permute_blk(far, to_core),
        permute_blk(all_near, to_core),
    )
    *begun, far_x = together(*forward(3, *begun, near_core, far_core), far_x)
    return together(*forward(4, *begun, far_x), permute_blk(far_x, to_core))


def behind(value, *others):
    corners = [other.reshape(-1, OWN)[:16, :TILE].astype(f32) for other in others]
    ins = [VMEM] * (1 + len(others))
    return call(copy_kernel, shape(value.shape, value.dtype), ins, cost=1 << 31)(value, *corners)


def scatter_terms(backward, grad):
    def rounded(value):
        return value.astype(f16).astype(f32)

    def with_grad(terms, grad):
        return jnp.concatenate([terms.reshape(-1, OWN), grad]).astype(f16)

    def parted(got, terms):
        n = terms.shape[0] * TILE
        got = got.astype(f32)
        return got[:n].reshape(terms.shape), got[n:]

    (give_far,) = backward(GIVE_FAR)
    (keep_far,) = backward(KEEP_FAR)
    far, more = parted(permute_blk(with_grad(give_far, grad), to_core), give_far)
    give_near, keep_near = backward(GIVE_NEAR, KEEP_NEAR)
    far, grad = keep_far + far, rounded(rounded(grad) + more)
    out = after(with_grad(far[:3], grad))
    mine = behind(grad, out).astype(f16)
    fan = [permute_blk(mine, to_z_xor(1, other_x)).astype(f32) for other_x in (0, 1)]
    far_x, more = parted(permute_blk(out, to_x), far[:3])
    near = keep_near + permute_blk(give_near.astype(f16), to_core).astype(f32)
    far = far[3:] + far_x
    grad = rounded((grad + more) + (fan[0] + fan[1]))
    out = after(with_grad(far, grad))
    near_out = after(near[:5].astype(f16))
    mine = behind(grad, out, near_out).astype(f16)
    grad = grad + permute_blk(mine, to_z_xor(4)).astype(f32)
    near_x = permute_blk(near_out, to_x).astype(f32)
    out = permute_blk(out, to_z_by_core(2))
    passed, more = parted(out, far)
    near = near[5:] + near_x
    two = jnp.concatenate([near[:1] + passed[:1], near[1:2]]).astype(f16)
    two, one = together(two, (near[2:4] + passed[1:]).astype(f16))
    mine = behind(more, two, one).astype(f16)
    grad = grad + (more + permute_blk(mine, to_core).astype(f32))
    grad = after(jnp.broadcast_to(grad.astype(f16)[None], (8, 32, 256)), two, one)
    got = permute_blk(two, to_z_by_core(2)).astype(f32) + permute_blk(one, to_z_by_core(1)).astype(f32)
    return near[4] + got[0], permute_blk(got[1].astype(f16), to_core).astype(f32), grad


def per_device(
    node_features,
    weight_matrix,
    bias_vector,
    node_degree,
    tile_values,
    tile_row,
    tile_count,
    cotangent,
):
    n_out = weight_matrix.shape[1]
    tiles = tile_values.reshape(-1, SLOTS * TILE, TILE)
    rows = tile_row.reshape(-1)
    count = tile_count.reshape(-1)
    degree = node_degree.reshape(OWN // TILE, TILE)
    place = lax.axis_index("blk").astype(jnp.int32).reshape(1)

    own, pair = call(
        scale_kernel,
        (shape((1, BLOCK, TILE), bf16), shape((2, BLOCK, TILE), bf16)),
        [HBM] * 3,
        [
            pltpu.VMEM((OWN, TILE), bf16),
            pltpu.VMEM((OWN // TILE, TILE), jnp.int32),
            pltpu.VMEM((OWN, n_out), bf16),
            pltpu.SemaphoreType.DMA((3,)),
        ],
        limit=None,
    )(node_features, degree, cotangent)
    acc = shape(((ROW_TILES + 1) * TILE, TILE), f32)
    marks = shape((BLOCK - OWN, TILE), f32)

    smem = (after(rows, own), after(count, own))

    def products(kernel, outs, scratch, *pieces):
        ins = [SMEM] * 3 + [VMEM] * (1 + len(pieces))
        return call(kernel, outs, ins, scratch, 1 << 29)(place, *smem, tiles, *pieces)

    def forward(step, *pieces):
        kernel = functools.partial(forward_kernel, FORWARD_ORDERS[step])
        return products(kernel, (acc, marks), [], *pieces)

    partial = products(
        forward_last_kernel,
        shape((8, BLOCK, TILE), f32),
        [pltpu.VMEM(acc.shape, f32)],
        *gather_blocks(own, pair, forward),
    )
    parts = lax.all_to_all(partial.astype(f16), "rep", 0, 0).astype(f32)
    hidden, back, grad, factor = call(
        middle_kernel,
        (
            shape((OWN, n_out), bf16),
            shape((TILE, OWN), f32),
            shape((8, 32, 256), f32),
            shape((2, 8, TILE), f32),
        ),
        [VMEM] * 6,
        cost=1 << 27,
    )(parts, weight_matrix, bias_vector.reshape(1, -1), degree, node_features, cotangent)

    sent = jnp.concatenate([jnp.broadcast_to(back[None], (8, TILE, OWN)), grad], 1).astype(f16)
    got = lax.all_to_all(sent, "rep", 0, 0).astype(f32)
    got_back = got[:, :TILE]

    def backward(*orders):
        return products(
            functools.partial(backward_kernel, orders),
            tuple(shape((len(order), TILE, OWN), f32) for order in orders),
            [pltpu.VMEM((ROW_TILES + 1, 2 * TILE, TILE), bf16)],
            got_back,
        )

    *halves, grad = scatter_terms(backward, jnp.sum(got[:, TILE:], 0))
    slices = lax.all_to_all(grad, "rep", 0, 0).astype(f32)
    input_grad, weight_grad = call(
        finish_kernel, (shape((OWN, TILE), bf16), shape((TILE, n_out), f32)), [VMEM] * 5
    )(*halves, degree, factor, slices)
    return hidden, weight_grad, input_grad


def solution(mesh):
    in_specs = (
        P(("blk", "rep"), None),
        P(),
        P(),
        P(("blk", "rep")),
        P("blk", "rep", None, None, None, None),
        P("blk", "rep", None, None),
        P("blk", "rep", None),
        P(("blk", "rep"), None),
    )
    out_specs = (P(("blk", "rep"), None), P(), P(("blk", "rep"), None))
    return jax.shard_map(
        per_device, mesh=mesh, in_specs=in_specs, out_specs=out_specs, check_vma=False
    )
```

```python
import functools

import jax
import jax.numpy as jnp
from jax import lax
from jax.experimental import pallas as pl
from jax.experimental.pallas import tpu as pltpu
from jax.sharding import PartitionSpec as P

f32, bf16, f16 = jnp.float32, jnp.bfloat16, jnp.float16

TILE = 128
OWN = 256
BLOCK = OWN + 16
N_X, N_Z, N_C = 2, 8, 2
N_Y = 4
SLOTS = 2
ROW_TILES = 16
VMEM_LIMIT = 16 * 1024 * 1024


def blk_index(x, z, c):
    return (x * N_Z + z) * N_C + c


def permute_blk(value, move):
    pairs = []
    for x in range(N_X):
        for z in range(N_Z):
            for c in range(N_C):
                pairs.append((blk_index(x, z, c), blk_index(*move(x, z, c))))
    return lax.ppermute(value, "blk", pairs)


def to_core(x, z, c):
    return x, z, 1 - c


def to_x(x, z, c):
    return 1 - x, z, c


def to_z_xor(bits, other_x=0):
    return lambda x, z, c: (x ^ other_x, z ^ bits, c)


def to_z_by_core(distance):
    return lambda x, z, c: (x, (z + (distance if c == 0 else -distance)) % N_Z, c)


def exponent_above(largest):
    return jnp.ceil(jnp.log2(jnp.maximum(largest, 1e-30))) + 1.0


def as_column(row):
    n = row.shape[1]
    diagonal = lax.broadcasted_iota(jnp.int32, (n, n), 0) == lax.broadcasted_iota(
        jnp.int32, (n, n), 1
    )
    return jnp.sum(jnp.where(diagonal, row, 0.0), axis=1, keepdims=True)


def scale_of(degree):
    scale = 1.0 / jnp.sqrt(degree.astype(f32))
    rows = [scale[i : i + 1, :] for i in range(scale.shape[0])]
    return jnp.concatenate(rows, 1), jnp.concatenate([as_column(r) for r in rows], 0)


def split(value):
    high = value.astype(bf16)
    return high, (value - high.astype(f32)).astype(bf16)


def scale_kernel(
    features_hbm, degree_hbm, cot_hbm, own_ref, pair_ref, features_ref, degree_ref, cot_ref, sems
):
    copies = [
        pltpu.make_async_copy(src, dst, sems.at[i])
        for i, (src, dst) in enumerate(
            [(degree_hbm, degree_ref), (features_hbm, features_ref), (cot_hbm, cot_ref)]
        )
    ]
    for copy in copies:
        copy.start()
    copies[0].wait()
    _, column = scale_of(degree_ref[...])
    copies[1].wait()
    scaled = (features_ref[...].astype(f32) * column).astype(bf16)
    own_ref[0, :OWN, :] = scaled
    copies[2].wait()
    cot = jnp.max(jnp.abs(cot_ref[...].astype(f32)))
    feature = jnp.max(jnp.abs(scaled.astype(f32)))
    rows = lax.broadcasted_iota(jnp.int32, (BLOCK - OWN, TILE), 0)
    own_ref[0, OWN:, :] = jnp.where(rows < 8, cot, feature).astype(bf16)
    pair_ref[0] = own_ref[0]
    pair_ref[1] = own_ref[0]


def column_block(at, dx, dz, dc):
    x, z, c = at // (N_Z * N_C), at // N_C % N_Z, at % N_C
    z = (z + N_Z + (1 - 2 * c) * dz) % N_Z
    return blk_index(x + dx - 2 * dx * x, z, c + dc - 2 * dc * c)


def add_products(order, place_ref, rows_ref, count_ref, tiles_ref, pieces, acc_ref):
    column_blocks = [
        column_block(place_ref[0], *block) for blocks in order for block in blocks
    ]
    refs = [(ref, at) for ref, blocks in zip(pieces, order, strict=True) for at in range(len(blocks))]
    largest = None
    for i, (ref, at) in enumerate(refs):
        marks = ref[at, OWN:, :].astype(f32)
        largest = marks if largest is None else jnp.maximum(largest, marks)
        for half in range(OWN // TILE):
            k = column_blocks[i] * (OWN // TILE) + half
            part = ref[at, half * TILE : (half + 1) * TILE, :]
            product = jnp.dot(tiles_ref[k], part, preferred_element_type=f32)
            for slot in range(SLOTS):
                row = rows_ref[k * SLOTS + slot]
                row = jnp.where(slot < count_ref[k], row, ROW_TILES)
                where = pl.ds(pl.multiple_of(row * TILE, TILE), TILE)
                acc_ref[where, :] += product[slot * TILE : (slot + 1) * TILE, :]
    return largest


def forward_kernel(order, place_ref, rows_ref, count_ref, tiles_ref, *refs):
    (acc_ref, marks_ref), refs = refs[-2:], refs[:-2]
    pieces = refs[-len(order) :]
    if len(refs) > len(order):
        acc_ref[...] = refs[0][...]
    else:
        acc_ref[...] = jnp.zeros_like(acc_ref)
    marks = add_products(order, place_ref, rows_ref, count_ref, tiles_ref, pieces, acc_ref)
    if len(refs) > len(order):
        marks = jnp.maximum(marks, refs[1][...])
    marks_ref[...] = marks


def forward_last_kernel(place_ref, rows_ref, count_ref, tiles_ref, begun_ref, begun_marks, *refs):
    pieces, (out_ref, acc_ref) = refs[:-2], refs[-2:]
    acc_ref[...] = begun_ref[...]
    largest = add_products(
        LAST_ORDER, place_ref, rows_ref, count_ref, tiles_ref, pieces, acc_ref
    )
    marks = exponent_above(jnp.maximum(largest, begun_marks[...]))
    shrink = 2.0 * jnp.exp2(-marks[8:9, :])
    for r in range(out_ref.shape[0]):
        out_ref[r, :OWN, :] = acc_ref[r * OWN : (r + 1) * OWN, :] * shrink
        out_ref[r, OWN:, :] = marks


FORWARD_ORDERS = [
    [[(0, 0, 0), (0, 0, 1)]],
    [[(1, 0, 0), (1, 0, 1)], [(0, -1, 0), (0, -1, 1), (0, -2, 0), (0, -2, 1)]],
    [[(1, -1, 0), (1, -1, 1), (1, -2, 0), (1, -2, 1)], [(0, -3, 0), (0, -3, 1), (0, 4, 0)]],
    [
        [(dx, i, dc) for dx in (0, 1) for i in (1, 2) for dc in (1, 0)],
        [(0, 3, 1), (0, 3, 0), (0, 4, 1)],
    ],
    [[(1, -3, 0), (1, -3, 1), (1, 4, 0)]],
]
LAST_ORDER = [[(1, 3, 1), (1, 3, 0), (1, 4, 1)]]


def middle_kernel(
    parts_ref,
    weight_ref,
    bias_ref,
    degree_ref,
    features_ref,
    cot_ref,
    hidden_ref,
    back_ref,
    grad_ref,
    factor_ref,
):
    row_scale, column_scale = scale_of(degree_ref[...])
    summed = jnp.zeros((OWN, TILE), f32)
    cot_mark = feature_mark = None
    for r in range(parts_ref.shape[0]):
        cot_r, feature_r = parts_ref[r, OWN : OWN + 1, :], parts_ref[r, OWN + 8 : OWN + 9, :]
        summed += parts_ref[r, :OWN, :] * (0.5 * jnp.exp2(feature_r))
        cot_mark = cot_r if cot_mark is None else jnp.maximum(cot_mark, cot_r)
        feature_mark = feature_r if feature_mark is None else jnp.maximum(feature_mark, feature_r)
    weight = weight_ref[...]
    high, low = split(summed)
    mixed = jnp.dot(high, weight, preferred_element_type=f32)
    mixed += jnp.dot(low, weight, preferred_element_type=f32)
    pre = column_scale * mixed + bias_ref[...]
    root = 0.7978845608028654
    square = pre * pre
    bent = jnp.tanh(root * pre * (1.0 + 0.044715 * square))
    half_up = 0.5 * (1.0 + bent)
    hidden_ref[...] = (pre * half_up).astype(bf16)
    slope = half_up + 0.5 * pre * (1.0 - bent * bent) * (root * (1.0 + 0.134145 * square))
    shrink = jnp.exp2(-cot_mark[:, :1])
    grad = cot_ref[...].astype(f32) * shrink * slope
    high, low = split(grad)
    across = (((1,), (1,)), ((), ()))
    back = lax.dot_general(weight, high, across, preferred_element_type=f32)
    back += lax.dot_general(weight, low, across, preferred_element_type=f32)
    weight_mark = exponent_above(jnp.max(jnp.abs(weight.astype(f32)), axis=(0, 1), keepdims=True))
    back_ref[...] = back * row_scale * (64.0 * jnp.exp2(-weight_mark))
    down = (((0,), (0,)), ((), ()))
    features = features_ref[...]
    local = lax.dot_general(features, high, down, preferred_element_type=f32)
    local += lax.dot_general(features, low, down, preferred_element_type=f32)
    local = local * (0.25 * jnp.exp2(-feature_mark[:, :1]))
    for i in range(N_Y):
        for j in range(2):
            part = local[i * 32 : (i + 1) * 32, j * 256 : (j + 1) * 256]
            grad_ref[i, j * 32 : (j + 1) * 32, :] = part
    one = jnp.ones((8, TILE), f32)
    factor_ref[0] = one * (16.0 * jnp.exp2(cot_mark + weight_mark))
    factor_ref[1] = one * (jnp.exp2(cot_mark + feature_mark) / 64.0)


def backward_kernel(orders, place_ref, rows_ref, count_ref, tiles_ref, back_ref, *refs):
    outs, group_ref = refs[:-1], refs[-1]
    for r in range(ROW_TILES):
        value = back_ref[r // 2, :, (r % 2) * TILE : (r % 2 + 1) * TILE] * (1.0 / 1024.0)
        high, low = split(value)
        group_ref[r, :TILE, :] = high
        group_ref[r, TILE:, :] = low
    group_ref[ROW_TILES] = jnp.zeros(group_ref.shape[1:], bf16)
    for ref, order in zip(outs, orders, strict=True):
        for at, block in enumerate(order):
            block = column_block(place_ref[0], *block)
            for half in range(OWN // TILE):
                k = block * (OWN // TILE) + half
                picked = []
                for slot in range(SLOTS):
                    row = rows_ref[k * SLOTS + slot]
                    picked.append(group_ref[jnp.where(slot < count_ref[k], row, ROW_TILES)])
                both = jnp.dot(
                    jnp.concatenate(picked, 1), tiles_ref[k], preferred_element_type=f32
                )
                ref[at, :, half * TILE : (half + 1) * TILE] = both[:TILE] + both[TILE:]


def join_kernel(first_ref, second_ref, _, out_ref):
    n = first_ref.shape[0]
    out_ref[:n] = first_ref[...]
    out_ref[n:] = second_ref[...]


def copy_kernel(value_ref, *refs):
    refs[-1][...] = value_ref[...]


def finish_kernel(mine_ref, theirs_ref, degree_ref, factor_ref, slices_ref, input_ref, weight_ref):
    factor = jnp.concatenate([factor_ref[1, :1, :]] * 2, 1)
    for i in range(N_Y):
        for j in range(2):
            part = slices_ref[i, j * 32 : (j + 1) * 32, :] * factor
            weight_ref[i * 32 : (i + 1) * 32, j * 256 : (j + 1) * 256] = part
    _, column_scale = scale_of(degree_ref[...])
    total = (mine_ref[...] + theirs_ref[...]).T
    input_ref[...] = (column_scale * total * factor_ref[0, :1, :]).astype(bf16)


GIVE_FAR = [(dx, *rest) for dx in (1, 0) for rest in ((4, 1), (-3, 1), (-3, 0))]
GIVE_NEAR = [(dx, *rest) for dx in (1, 0) for rest in ((-2, 1), (-2, 0), (-1, 1), (-1, 0), (0, 1))]
KEEP_FAR = [(dx, *rest) for dx in (1, 0) for rest in ((4, 0), (3, 0), (3, 1))]
KEEP_NEAR = [(dx, *rest) for dx in (1, 0) for rest in ((2, 0), (2, 1), (1, 0), (1, 1), (0, 0))]


SMEM = pl.BlockSpec(memory_space=pltpu.SMEM)
VMEM = pl.BlockSpec(memory_space=pltpu.VMEM)
HBM = pl.BlockSpec(memory_space=pltpu.HBM)


def shape(dims, dtype):
    return jax.ShapeDtypeStruct(dims, dtype)


def call(kernel, outs, ins, scratch=(), cost=0, limit=VMEM_LIMIT):
    return pl.pallas_call(
        kernel,
        out_shape=outs,
        in_specs=ins,
        out_specs=jax.tree.map(lambda _: VMEM, outs),
        scratch_shapes=list(scratch),
        compiler_params=pltpu.CompilerParams(vmem_limit_bytes=limit),
        cost_estimate=pl.CostEstimate(flops=cost, bytes_accessed=1 << 20, transcendentals=0),
    )


def after(value, *others):
    return lax.optimization_barrier((value, *others))[0]


def together(*values):
    return lax.optimization_barrier(values)


def gather_blocks(own, pair, forward):
    pair = lax.dynamic_update_slice(pair, permute_blk(own, to_core), (1, 0, 0))
    *begun, near_2, near_1, pair_x = together(
        *forward(0, pair),
        permute_blk(pair, to_z_by_core(2)),
        permute_blk(pair, to_z_by_core(1)),
        permute_blk(pair, to_x),
    )
    near = jnp.concatenate([near_1, near_2])
    *begun, far, near_x = together(
        *forward(1, *begun, pair_x, near),
        permute_blk(near[:3], to_z_by_core(2)),
        permute_blk(near, to_x),
    )
    far_x = permute_blk(far, to_x)
    all_near = call(join_kernel, shape((8, BLOCK, TILE), bf16), [VMEM] * 3, cost=1 << 31)(
        near, near_x, far
    )
    *begun, far_core, near_core = together(
        *forward(2, *begun, near_x, far),
        permute_blk(far, to_core),
        permute_blk(all_near, to_core),
    )
    *begun, far_x = together(*forward(3, *begun, near_core, far_core), far_x)
    return together(*forward(4, *begun, far_x), permute_blk(far_x, to_core))


def behind(value, *others):
    corners = [other.reshape(-1, OWN)[:16, :TILE].astype(f32) for other in others]
    ins = [VMEM] * (1 + len(others))
    return call(copy_kernel, shape(value.shape, value.dtype), ins, cost=1 << 31)(value, *corners)


def scatter_terms(backward, grad):
    def rounded(value):
        return value.astype(f16).astype(f32)

    def with_grad(terms, grad):
        return jnp.concatenate([terms.reshape(-1, OWN), grad]).astype(f16)

    def parted(got, terms):
        n = terms.shape[0] * TILE
        got = got.astype(f32)
        return got[:n].reshape(terms.shape), got[n:]

    (give_far,) = backward(GIVE_FAR)
    (keep_far,) = backward(KEEP_FAR)
    far, more = parted(permute_blk(with_grad(give_far, grad), to_core), give_far)
    give_near, keep_near = backward(GIVE_NEAR, KEEP_NEAR)
    far, grad = keep_far + far, rounded(rounded(grad) + more)
    out = after(with_grad(far[:3], grad))
    mine = behind(grad, out).astype(f16)
    fan = [permute_blk(mine, to_z_xor(1, other_x)).astype(f32) for other_x in (0, 1)]
    far_x, more = parted(permute_blk(out, to_x), far[:3])
    near = keep_near + permute_blk(give_near.astype(f16), to_core).astype(f32)
    far = far[3:] + far_x
    grad = rounded((grad + more) + (fan[0] + fan[1]))
    out = after(with_grad(far, grad))
    near_out = after(near[:5].astype(f16))
    mine = behind(grad, out, near_out).astype(f16)
    grad = grad + permute_blk(mine, to_z_xor(4)).astype(f32)
    near_x = permute_blk(near_out, to_x).astype(f32)
    out = permute_blk(out, to_z_by_core(2))
    passed, more = parted(out, far)
    near = near[5:] + near_x
    two = jnp.concatenate([near[:1] + passed[:1], near[1:2]]).astype(f16)
    two, one = together(two, (near[2:4] + passed[1:]).astype(f16))
    mine = behind(more, two, one).astype(f16)
    grad = grad + (more + permute_blk(mine, to_core).astype(f32))
    grad = after(jnp.broadcast_to(grad.astype(f16)[None], (N_Y, 64, 256)), two, one)
    got = permute_blk(two, to_z_by_core(2)).astype(f32) + permute_blk(one, to_z_by_core(1)).astype(f32)
    return near[4] + got[0], permute_blk(got[1].astype(f16), to_core).astype(f32), grad


def per_device(
    node_features,
    weight_matrix,
    bias_vector,
    node_degree,
    tile_values,
    tile_row,
    tile_count,
    cotangent,
):
    n_out = weight_matrix.shape[1]
    tiles = tile_values.reshape(-1, SLOTS * TILE, TILE)
    rows = tile_row.reshape(-1)
    count = tile_count.reshape(-1)
    degree = node_degree.reshape(OWN // TILE, TILE)
    place = lax.axis_index("blk").astype(jnp.int32).reshape(1)

    own, pair = call(
        scale_kernel,
        (shape((1, BLOCK, TILE), bf16), shape((2, BLOCK, TILE), bf16)),
        [HBM] * 3,
        [
            pltpu.VMEM((OWN, TILE), bf16),
            pltpu.VMEM((OWN // TILE, TILE), jnp.int32),
            pltpu.VMEM((OWN, n_out), bf16),
            pltpu.SemaphoreType.DMA((3,)),
        ],
        limit=None,
    )(node_features, degree, cotangent)
    acc = shape(((ROW_TILES + 1) * TILE, TILE), f32)
    marks = shape((BLOCK - OWN, TILE), f32)

    smem = (after(rows, own), after(count, own))

    def products(kernel, outs, scratch, *pieces):
        ins = [SMEM] * 3 + [VMEM] * (1 + len(pieces))
        return call(kernel, outs, ins, scratch, 1 << 29)(place, *smem, tiles, *pieces)

    def forward(step, *pieces):
        kernel = functools.partial(forward_kernel, FORWARD_ORDERS[step])
        return products(kernel, (acc, marks), [], *pieces)

    partial = products(
        forward_last_kernel,
        shape((8, BLOCK, TILE), f32),
        [pltpu.VMEM(acc.shape, f32)],
        *gather_blocks(own, pair, forward),
    )
    parts = lax.all_to_all(partial.astype(f16), "rep", 0, 0).astype(f32)
    hidden, back, grad, factor = call(
        middle_kernel,
        (
            shape((OWN, n_out), bf16),
            shape((TILE, OWN), f32),
            shape((N_Y, 64, 256), f32),
            shape((2, 8, TILE), f32),
        ),
        [VMEM] * 6,
        cost=1 << 27,
    )(parts, weight_matrix, bias_vector.reshape(1, -1), degree, node_features, cotangent)

    sent = jnp.concatenate([jnp.broadcast_to(back[None], (8, TILE, OWN)), jnp.concatenate([grad, grad])], 1).astype(f16)
    got = lax.all_to_all(sent, "rep", 0, 0).astype(f32)
    got_back = got[:, :TILE]

    def backward(*orders):
        return products(
            functools.partial(backward_kernel, orders),
            tuple(shape((len(order), TILE, OWN), f32) for order in orders),
            [pltpu.VMEM((ROW_TILES + 1, 2 * TILE, TILE), bf16)],
            got_back,
        )

    *halves, grad = scatter_terms(backward, jnp.sum(got[:, TILE:], 0))
    along_y = [list(range(N_Y)), list(range(N_Y, 2 * N_Y))]
    slices = lax.all_to_all(grad, "rep", 0, 0, axis_index_groups=along_y).astype(f32)
    input_grad, weight_grad = call(
        finish_kernel, (shape((OWN, TILE), bf16), shape((TILE, n_out), f32)), [VMEM] * 5
    )(*halves, degree, factor, slices)
    return hidden, weight_grad, input_grad


def solution(mesh):
    in_specs = (
        P(("blk", "rep"), None),
        P(),
        P(),
        P(("blk", "rep")),
        P("blk", "rep", None, None, None, None),
        P("blk", "rep", None, None),
        P("blk", "rep", None),
        P(("blk", "rep"), None),
    )
    out_specs = (P(("blk", "rep"), None), P(), P(("blk", "rep"), None))
    return jax.shard_map(
        per_device, mesh=mesh, in_specs=in_specs, out_specs=out_specs, check_vma=False
    )
```

```python
import functools

import jax
import jax.numpy as jnp
from jax import lax
from jax.experimental import pallas as pl
from jax.experimental.pallas import tpu as pltpu
from jax.sharding import PartitionSpec as P

f32, bf16, f16 = jnp.float32, jnp.bfloat16, jnp.float16

TILE = 128
OWN = 256
BLOCK = OWN + 16
N_X, N_Z, N_C = 2, 8, 2
N_Y = 4
SLOTS = 2
ROW_TILES = 16
VMEM_LIMIT = 16 * 1024 * 1024


def blk_index(x, z, c):
    return (x * N_Z + z) * N_C + c


def permute_blk(value, move):
    pairs = []
    for x in range(N_X):
        for z in range(N_Z):
            for c in range(N_C):
                pairs.append((blk_index(x, z, c), blk_index(*move(x, z, c))))
    return lax.ppermute(value, "blk", pairs)


def to_core(x, z, c):
    return x, z, 1 - c


def to_x(x, z, c):
    return 1 - x, z, c


def to_z_xor(bits, other_x=0):
    return lambda x, z, c: (x ^ other_x, z ^ bits, c)


def to_z_by_core(distance):
    return lambda x, z, c: (x, (z + (distance if c == 0 else -distance)) % N_Z, c)


def exponent_above(largest):
    return jnp.ceil(jnp.log2(jnp.maximum(largest, 1e-30))) + 1.0


def as_column(row):
    n = row.shape[1]
    diagonal = lax.broadcasted_iota(jnp.int32, (n, n), 0) == lax.broadcasted_iota(
        jnp.int32, (n, n), 1
    )
    return jnp.sum(jnp.where(diagonal, row, 0.0), axis=1, keepdims=True)


def scale_of(degree):
    scale = 1.0 / jnp.sqrt(degree.astype(f32))
    rows = [scale[i : i + 1, :] for i in range(scale.shape[0])]
    return jnp.concatenate(rows, 1), jnp.concatenate([as_column(r) for r in rows], 0)


def split(value):
    high = value.astype(bf16)
    return high, (value - high.astype(f32)).astype(bf16)


def scale_kernel(
    features_hbm, degree_hbm, cot_hbm, own_ref, pair_ref, features_ref, degree_ref, cot_ref, sems
):
    copies = [
        pltpu.make_async_copy(src, dst, sems.at[i])
        for i, (src, dst) in enumerate(
            [(degree_hbm, degree_ref), (features_hbm, features_ref), (cot_hbm, cot_ref)]
        )
    ]
    for copy in copies:
        copy.start()
    copies[0].wait()
    _, column = scale_of(degree_ref[...])
    copies[1].wait()
    scaled = (features_ref[...].astype(f32) * column).astype(bf16)
    own_ref[0, :OWN, :] = scaled
    copies[2].wait()
    cot = jnp.max(jnp.abs(cot_ref[...].astype(f32)))
    feature = jnp.max(jnp.abs(scaled.astype(f32)))
    rows = lax.broadcasted_iota(jnp.int32, (BLOCK - OWN, TILE), 0)
    own_ref[0, OWN:, :] = jnp.where(rows < 8, cot, feature).astype(bf16)
    pair_ref[0] = own_ref[0]
    pair_ref[1] = own_ref[0]


def column_block(at, dx, dz, dc):
    x, z, c = at // (N_Z * N_C), at // N_C % N_Z, at % N_C
    z = (z + N_Z + (1 - 2 * c) * dz) % N_Z
    return blk_index(x + dx - 2 * dx * x, z, c + dc - 2 * dc * c)


def add_products(order, place_ref, rows_ref, count_ref, tiles_ref, pieces, acc_ref):
    column_blocks = [
        column_block(place_ref[0], *block) for blocks in order for block in blocks
    ]
    refs = [(ref, at) for ref, blocks in zip(pieces, order, strict=True) for at in range(len(blocks))]
    largest = None
    for i, (ref, at) in enumerate(refs):
        marks = ref[at, OWN:, :].astype(f32)
        largest = marks if largest is None else jnp.maximum(largest, marks)
        for half in range(OWN // TILE):
            k = column_blocks[i] * (OWN // TILE) + half
            part = ref[at, half * TILE : (half + 1) * TILE, :]
            product = jnp.dot(tiles_ref[k], part, preferred_element_type=f32)
            for slot in range(SLOTS):
                row = rows_ref[k * SLOTS + slot]
                row = jnp.where(slot < count_ref[k], row, ROW_TILES)
                where = pl.ds(pl.multiple_of(row * TILE, TILE), TILE)
                acc_ref[where, :] += product[slot * TILE : (slot + 1) * TILE, :]
    return largest


def forward_kernel(order, place_ref, rows_ref, count_ref, tiles_ref, *refs):
    (acc_ref, marks_ref), refs = refs[-2:], refs[:-2]
    pieces = refs[-len(order) :]
    if len(refs) > len(order):
        acc_ref[...] = refs[0][...]
    else:
        acc_ref[...] = jnp.zeros_like(acc_ref)
    marks = add_products(order, place_ref, rows_ref, count_ref, tiles_ref, pieces, acc_ref)
    if len(refs) > len(order):
        marks = jnp.maximum(marks, refs[1][...])
    marks_ref[...] = marks


def forward_last_kernel(place_ref, rows_ref, count_ref, tiles_ref, begun_ref, begun_marks, *refs):
    pieces, (out_ref, acc_ref) = refs[:-2], refs[-2:]
    acc_ref[...] = begun_ref[...]
    largest = add_products(
        LAST_ORDER, place_ref, rows_ref, count_ref, tiles_ref, pieces, acc_ref
    )
    marks = exponent_above(jnp.maximum(largest, begun_marks[...]))
    shrink = 2.0 * jnp.exp2(-marks[8:9, :])
    for r in range(out_ref.shape[0]):
        out_ref[r, :OWN, :] = acc_ref[r * OWN : (r + 1) * OWN, :] * shrink
        out_ref[r, OWN:, :] = marks


FORWARD_ORDERS = [
    [[(0, 0, 0), (0, 0, 1)]],
    [[(1, 0, 0), (1, 0, 1)], [(0, -1, 0), (0, -1, 1), (0, -2, 0), (0, -2, 1)]],
    [[(1, -1, 0), (1, -1, 1), (1, -2, 0), (1, -2, 1)], [(0, -3, 0), (0, -3, 1), (0, 4, 0)]],
    [
        [(dx, i, dc) for dx in (0, 1) for i in (1, 2) for dc in (1, 0)],
    ],
    [[(1, -3, 0), (1, -3, 1), (1, 4, 0)]],
]
LAST_ORDER = [[(dx, *rest) for dx in (0, 1) for rest in ((3, 1), (3, 0), (4, 1))]]


def middle_kernel(
    parts_ref,
    weight_ref,
    bias_ref,
    degree_ref,
    features_ref,
    cot_ref,
    hidden_ref,
    back_ref,
    grad_ref,
    factor_ref,
):
    row_scale, column_scale = scale_of(degree_ref[...])
    summed = jnp.zeros((OWN, TILE), f32)
    cot_mark = feature_mark = None
    for r in range(parts_ref.shape[0]):
        cot_r, feature_r = parts_ref[r, OWN : OWN + 1, :], parts_ref[r, OWN + 8 : OWN + 9, :]
        summed += parts_ref[r, :OWN, :] * (0.5 * jnp.exp2(feature_r))
        cot_mark = cot_r if cot_mark is None else jnp.maximum(cot_mark, cot_r)
        feature_mark = feature_r if feature_mark is None else jnp.maximum(feature_mark, feature_r)
    weight = weight_ref[...]
    high, low = split(summed)
    mixed = jnp.dot(high, weight, preferred_element_type=f32)
    mixed += jnp.dot(low, weight, preferred_element_type=f32)
    pre = column_scale * mixed + bias_ref[...]
    root = 0.7978845608028654
    square = pre * pre
    bent = jnp.tanh(root * pre * (1.0 + 0.044715 * square))
    half_up = 0.5 * (1.0 + bent)
    hidden_ref[...] = (pre * half_up).astype(bf16)
    slope = half_up + 0.5 * pre * (1.0 - bent * bent) * (root * (1.0 + 0.134145 * square))
    shrink = jnp.exp2(-cot_mark[:, :1])
    grad = cot_ref[...].astype(f32) * shrink * slope
    high, low = split(grad)
    across = (((1,), (1,)), ((), ()))
    back = lax.dot_general(weight, high, across, preferred_element_type=f32)
    back += lax.dot_general(weight, low, across, preferred_element_type=f32)
    weight_mark = exponent_above(jnp.max(jnp.abs(weight.astype(f32)), axis=(0, 1), keepdims=True))
    back_ref[...] = back * row_scale * (64.0 * jnp.exp2(-weight_mark))
    down = (((0,), (0,)), ((), ()))
    features = features_ref[...]
    local = lax.dot_general(features, high, down, preferred_element_type=f32)
    local += lax.dot_general(features, low, down, preferred_element_type=f32)
    local = local * (0.25 * jnp.exp2(-feature_mark[:, :1]))
    for r in range(grad_ref.shape[0]):
        i, j = r // 2, r % 2
        grad_ref[r] = local[i * 32 : (i + 1) * 32, j * 256 : (j + 1) * 256]
    one = jnp.ones((8, TILE), f32)
    factor_ref[0] = one * (16.0 * jnp.exp2(cot_mark + weight_mark))
    factor_ref[1] = one * (jnp.exp2(cot_mark + feature_mark) / 64.0)


def backward_kernel(orders, place_ref, rows_ref, count_ref, tiles_ref, back_ref, *refs):
    outs, group_ref = refs[:-1], refs[-1]
    for r in range(ROW_TILES):
        value = back_ref[r // 2, :, (r % 2) * TILE : (r % 2 + 1) * TILE] * (1.0 / 1024.0)
        high, low = split(value)
        group_ref[r, :TILE, :] = high
        group_ref[r, TILE:, :] = low
    group_ref[ROW_TILES] = jnp.zeros(group_ref.shape[1:], bf16)
    for ref, order in zip(outs, orders, strict=True):
        for at, block in enumerate(order):
            block = column_block(place_ref[0], *block)
            for half in range(OWN // TILE):
                k = block * (OWN // TILE) + half
                picked = []
                for slot in range(SLOTS):
                    row = rows_ref[k * SLOTS + slot]
                    picked.append(group_ref[jnp.where(slot < count_ref[k], row, ROW_TILES)])
                both = jnp.dot(
                    jnp.concatenate(picked, 1), tiles_ref[k], preferred_element_type=f32
                )
                ref[at, :, half * TILE : (half + 1) * TILE] = both[:TILE] + both[TILE:]


def join_kernel(first_ref, second_ref, _, out_ref):
    n = first_ref.shape[0]
    out_ref[:n] = first_ref[...]
    out_ref[n:] = second_ref[...]


def copy_kernel(value_ref, *refs):
    refs[-1][...] = value_ref[...]


def finish_kernel(mine_ref, theirs_ref, degree_ref, factor_ref, slices_ref, input_ref, weight_ref):
    factor = jnp.concatenate([factor_ref[1, :1, :]] * 2, 1)
    for r in range(slices_ref.shape[0]):
        i, j = r // 2, r % 2
        weight_ref[i * 32 : (i + 1) * 32, j * 256 : (j + 1) * 256] = slices_ref[r] * factor
    _, column_scale = scale_of(degree_ref[...])
    total = (mine_ref[...] + theirs_ref[...]).T
    input_ref[...] = (column_scale * total * factor_ref[0, :1, :]).astype(bf16)


GIVE_FAR = [(dx, *rest) for dx in (1, 0) for rest in ((4, 1), (-3, 1), (-3, 0))]
GIVE_NEAR = [(dx, *rest) for dx in (1, 0) for rest in ((-2, 1), (-2, 0), (-1, 1), (-1, 0), (0, 1))]
KEEP_FAR = [(dx, *rest) for dx in (1, 0) for rest in ((4, 0), (3, 0), (3, 1))]
KEEP_NEAR = [(dx, *rest) for dx in (1, 0) for rest in ((2, 0), (2, 1), (1, 0), (1, 1), (0, 0))]


SMEM = pl.BlockSpec(memory_space=pltpu.SMEM)
VMEM = pl.BlockSpec(memory_space=pltpu.VMEM)
HBM = pl.BlockSpec(memory_space=pltpu.HBM)


def shape(dims, dtype):
    return jax.ShapeDtypeStruct(dims, dtype)


def call(kernel, outs, ins, scratch=(), cost=0, limit=VMEM_LIMIT):
    return pl.pallas_call(
        kernel,
        out_shape=outs,
        in_specs=ins,
        out_specs=jax.tree.map(lambda _: VMEM, outs),
        scratch_shapes=list(scratch),
        compiler_params=pltpu.CompilerParams(vmem_limit_bytes=limit),
        cost_estimate=pl.CostEstimate(flops=cost, bytes_accessed=1 << 20, transcendentals=0),
    )


def after(value, *others):
    return lax.optimization_barrier((value, *others))[0]


def together(*values):
    return lax.optimization_barrier(values)


def gather_blocks(own, pair, forward):
    pair = lax.dynamic_update_slice(pair, permute_blk(own, to_core), (1, 0, 0))
    *begun, near_2, near_1, pair_x = together(
        *forward(0, pair),
        permute_blk(pair, to_z_by_core(2)),
        permute_blk(pair, to_z_by_core(1)),
        permute_blk(pair, to_x),
    )
    near = jnp.concatenate([near_1, near_2])
    *begun, far, near_x = together(
        *forward(1, *begun, pair_x, near),
        permute_blk(near[:3], to_z_by_core(2)),
        permute_blk(near, to_x),
    )
    far_x = permute_blk(far, to_x)
    all_near = call(join_kernel, shape((8, BLOCK, TILE), bf16), [VMEM] * 3, cost=1 << 31)(
        near, near_x, far
    )
    *begun, near_core = together(
        *forward(2, *begun, near_x, far), permute_blk(all_near, to_core)
    )
    *begun, far_x = together(*forward(3, *begun, near_core), far_x)
    far_core = permute_blk(jnp.concatenate([far, far_x]), to_core)
    return together(*forward(4, *begun, far_x), far_core)


def behind(value, *others):
    corners = [other.reshape(-1, OWN)[:16, :TILE].astype(f32) for other in others]
    ins = [VMEM] * (1 + len(others))
    return call(copy_kernel, shape(value.shape, value.dtype), ins, cost=1 << 31)(value, *corners)


def scatter_terms(backward, grad):
    def rounded(value):
        return value.astype(f16).astype(f32)

    def with_grad(terms, grad):
        return jnp.concatenate([terms.reshape(-1, OWN), grad]).astype(f16)

    def parted(got, terms):
        n = terms.shape[0] * TILE
        got = got.astype(f32)
        return got[:n].reshape(terms.shape), got[n:]

    (give_far,) = backward(GIVE_FAR)
    (keep_far,) = backward(KEEP_FAR)
    far, more = parted(permute_blk(with_grad(give_far, grad), to_core), give_far)
    give_near, keep_near = backward(GIVE_NEAR, KEEP_NEAR)
    far, grad = keep_far + far, rounded(rounded(grad) + more)
    out = after(with_grad(far[:3], grad))
    mine = behind(grad, out).astype(f16)
    fan = [permute_blk(mine, to_z_xor(1, other_x)).astype(f32) for other_x in (0, 1)]
    far_x, more = parted(permute_blk(out, to_x), far[:3])
    near = keep_near + permute_blk(give_near.astype(f16), to_core).astype(f32)
    far = far[3:] + far_x
    grad = rounded((grad + more) + (fan[0] + fan[1]))
    out = after(with_grad(far, grad))
    near_out = after(near[:5].astype(f16))
    mine = behind(grad, out, near_out).astype(f16)
    grad = grad + permute_blk(mine, to_z_xor(4)).astype(f32)
    near_x = permute_blk(near_out, to_x).astype(f32)
    out = permute_blk(out, to_z_by_core(2))
    passed, more = parted(out, far)
    near = near[5:] + near_x
    two = jnp.concatenate([near[:1] + passed[:1], near[1:2]]).astype(f16)
    two, one = together(two, (near[2:4] + passed[1:]).astype(f16))
    mine = behind(more, two, one).astype(f16)
    grad = grad + (more + permute_blk(mine, to_core).astype(f32))
    grad = after(jnp.broadcast_to(grad.astype(f16)[None], (8, 32, 256)), two, one)
    got = permute_blk(two, to_z_by_core(2)).astype(f32) + permute_blk(one, to_z_by_core(1)).astype(f32)
    return near[4] + got[0], permute_blk(got[1].astype(f16), to_core).astype(f32), grad


def per_device(
    node_features,
    weight_matrix,
    bias_vector,
    node_degree,
    tile_values,
    tile_row,
    tile_count,
    cotangent,
):
    n_out = weight_matrix.shape[1]
    tiles = tile_values.reshape(-1, SLOTS * TILE, TILE)
    rows = tile_row.reshape(-1)
    count = tile_count.reshape(-1)
    degree = node_degree.reshape(OWN // TILE, TILE)
    place = lax.axis_index("blk").astype(jnp.int32).reshape(1)

    own, pair = call(
        scale_kernel,
        (shape((1, BLOCK, TILE), bf16), shape((2, BLOCK, TILE), bf16)),
        [HBM] * 3,
        [
            pltpu.VMEM((OWN, TILE), bf16),
            pltpu.VMEM((OWN // TILE, TILE), jnp.int32),
            pltpu.VMEM((OWN, n_out), bf16),
            pltpu.SemaphoreType.DMA((3,)),
        ],
        limit=None,
    )(node_features, degree, cotangent)
    acc = shape(((ROW_TILES + 1) * TILE, TILE), f32)
    marks = shape((BLOCK - OWN, TILE), f32)

    smem = (after(rows, own), after(count, own))

    def products(kernel, outs, scratch, *pieces):
        ins = [SMEM] * 3 + [VMEM] * (1 + len(pieces))
        return call(kernel, outs, ins, scratch, 1 << 29)(place, *smem, tiles, *pieces)

    def forward(step, *pieces):
        kernel = functools.partial(forward_kernel, FORWARD_ORDERS[step])
        return products(kernel, (acc, marks), [], *pieces)

    partial = products(
        forward_last_kernel,
        shape((8, BLOCK, TILE), f32),
        [pltpu.VMEM(acc.shape, f32)],
        *gather_blocks(own, pair, forward),
    )
    parts = lax.all_to_all(partial.astype(f16), "rep", 0, 0).astype(f32)
    hidden, back, grad, factor = call(
        middle_kernel,
        (
            shape((OWN, n_out), bf16),
            shape((TILE, OWN), f32),
            shape((8, 32, 256), f32),
            shape((2, 8, TILE), f32),
        ),
        [VMEM] * 6,
        cost=1 << 27,
    )(parts, weight_matrix, bias_vector.reshape(1, -1), degree, node_features, cotangent)

    sent = jnp.concatenate([jnp.broadcast_to(back[None], (8, TILE, OWN)), grad], 1).astype(f16)
    got = lax.all_to_all(sent, "rep", 0, 0).astype(f32)
    got_back = got[:, :TILE]

    def backward(*orders):
        return products(
            functools.partial(backward_kernel, orders),
            tuple(shape((len(order), TILE, OWN), f32) for order in orders),
            [pltpu.VMEM((ROW_TILES + 1, 2 * TILE, TILE), bf16)],
            got_back,
        )

    *halves, grad = scatter_terms(backward, jnp.sum(got[:, TILE:], 0))
    slices = lax.all_to_all(grad, "rep", 0, 0).astype(f32)
    input_grad, weight_grad = call(
        finish_kernel, (shape((OWN, TILE), bf16), shape((TILE, n_out), f32)), [VMEM] * 5
    )(*halves, degree, factor, slices)
    return hidden, weight_grad, input_grad


def solution(mesh):
    in_specs = (
        P(("blk", "rep"), None),
        P(),
        P(),
        P(("blk", "rep")),
        P("blk", "rep", None, None, None, None),
        P("blk", "rep", None, None),
        P("blk", "rep", None),
        P(("blk", "rep"), None),
    )
    out_specs = (P(("blk", "rep"), None), P(), P(("blk", "rep"), None))
    return jax.shard_map(
        per_device, mesh=mesh, in_specs=in_specs, out_specs=out_specs, check_vma=False
    )
```
